128 devices in a mesh: row: 16 (over z_hi, y, core), col: 8 (over z_lo, x).
Axes of the slice: x: 4, y: 4, z: 4 (z_hi: 2, z_lo: 2; z = z_hi * 2 + z_lo), core: 2. Of those that a mesh axis runs over, the one named last changes fastest.
Arguments:
- token_ids: int32 [16384], P(('row', 'col')), may hold values from 0 to 511
- embedding: bfloat16 [512, 8192], replicated, may hold values from -6 to 6
- norm_gain: bfloat16 [8192], replicated, may hold values from 0.099609375 to 1.8984375
- w_in: bfloat16 [8192, 12288], P(None, ('row', 'col')), may hold values from -0.0625 to 0.0625
- short_taps: float32 [7, 12288], replicated, may hold values from -2 to 2
- long_filter: float32 [16384, 4096], P(('row', 'col')), may hold values from -0.046875 to 0.046875
- skip_gain: float32 [4096], replicated, may hold values from -1 to 1
Outputs:
- mixed_out: bfloat16 [16384, 4096], P(('row', 'col'))
The draws below stay inside these ranges and needn't reach their ends.
All inputs are finite; a program needn't handle non-finite values.
Results may differ from the reference program's by a relative error of at most 0.0095.
Values may be sent and summed in bfloat16 or wider, within the bound.
No kernel may reach another device: no remote copies, remote signals or barrier semaphores. Data moves between devices by JAX's collectives and lax.ppermute only.
A program may use at most 192 MiB of HBM per device.

```python
import math
import jax
import jax.numpy as jnp
import numpy as np
from jax import lax

D = 8192
VOCAB = 512
CH = 4096
TAPS = 7
SEQ = 16384


def place_ends(entries, stream_key, low, high):
    longest = entries.shape.index(max(entries.shape))
    spots = []
    for shift in (0, 1):
        where = [jax.random.randint(jax.random.fold_in(stream_key, axis), (), 0, length) for axis, length in enumerate(entries.shape)]
        where[longest] = (where[longest] + shift) % entries.shape[longest]
        spots.append(tuple(where))
    return entries.at[spots[0]].set(low).at[spots[1]].set(high)


def levels(stream_key, dims, shards, low, top_value):
    gain = 1.0
    for axis_at, blocks in shards:
        steps = jax.random.uniform(jax.random.fold_in(jax.random.fold_in(stream_key, 6), axis_at), (blocks,), jnp.float32, low / len(shards), top_value / len(shards))
        gain = gain * jnp.repeat(jnp.exp(steps), dims[axis_at] // blocks).reshape((-1,) + (1,) * (len(dims) - 1 - axis_at))
    return gain


def rank_table(number_of, slope):
    loads = [(1 << 20) // math.isqrt(grade ** slope) + 1 for grade in range(1, number_of + 1)]
    spread = 1 + sum(loads) // (1 << 30)
    return np.cumsum(np.array([max(1, weight // spread) for weight in loads]))


def ranked_ids(key, extent, number_of, lean):
    table = rank_table(number_of, lean)
    ticket = jax.random.randint(jax.random.fold_in(key, 1), extent, 0, int(table[number_of - 1]))
    standing = jnp.searchsorted(jnp.asarray(table, jnp.int32), ticket, side="right")
    return jax.random.permutation(jax.random.fold_in(key, 2), number_of)[standing].astype(jnp.int32)


def bell_draw(stream_key, extent, scale, limit, split=(), dtype=jnp.bfloat16):
    entries = jax.random.normal(stream_key, extent, jnp.float32) * scale
    if len(split) > 0:
        entries = levels(stream_key, extent, split, -0.22, 0.18) * entries
    return jnp.clip(entries, min=-limit, max=limit).astype(dtype)


def setup_inputs(seed: int = 0) -> dict:
    key_list = jax.random.split(jax.random.key(seed), 8)
    return {
        "token_ids": place_ends(ranked_ids(key_list[0], (SEQ,), VOCAB, 2), jax.random.fold_in(key_list[0], 3), 0, VOCAB - 1).astype(jnp.int32),
        "embedding": bell_draw(key_list[1], (VOCAB, D), 1.0, 6.0),
        "norm_gain": jnp.clip(1.0 + 0.18 * jax.random.normal(key_list[2], (D,), jnp.float32), 0.099609375, 1.8984375).astype(jnp.bfloat16),
        "w_in": bell_draw(key_list[3], (D, 3 * CH), D ** -0.5, 0.0625, ((1, 128),)),
        "short_taps": bell_draw(key_list[4], (TAPS, 3 * CH), TAPS ** -0.5, 2.0, (), jnp.float32),
        "long_filter": bell_draw(key_list[5], (SEQ, CH), SEQ ** -0.5, 0.046875, ((0, 128),), jnp.float32),
        "skip_gain": jnp.clip(jax.random.uniform(key_list[6], (CH,), jnp.float32, -1.0, 1.0), -1.0, 1.0),
    }


EPSILON = 1e-05

def reference(token_ids, embedding, norm_gain, w_in, short_taps, long_filter, skip_gain):
    rows_f32 = embedding.astype(jnp.float32)
    inverse_rms = lax.rsqrt(lax.optimization_barrier(jnp.mean(rows_f32 * rows_f32, axis=1, keepdims=True)) + EPSILON)
    normed = (rows_f32 * inverse_rms * norm_gain.astype(jnp.float32)).astype(jnp.bfloat16)
    lookup_table = jnp.dot(normed, w_in, preferred_element_type=jnp.float32).astype(jnp.bfloat16)
    mixed_rows = jnp.take(lookup_table, token_ids, axis=0)
    tap_count = short_taps.shape[0]
    row_count = mixed_rows.shape[0]
    padding = jnp.zeros((tap_count - 1, mixed_rows.shape[1]), jnp.float32)
    extended = jnp.concatenate([padding, mixed_rows.astype(jnp.float32)], axis=0)
    weights = short_taps.astype(jnp.float32)
    filtered = weights[0] * extended[tap_count - 1:]
    for offset in range(1, tap_count):
        begin_at = tap_count - 1 - offset
        filtered = filtered + weights[offset] * extended[begin_at:begin_at + row_count]
    channels = filtered.shape[1] // 3
    gate_out = filtered[:, :channels]
    gate_in = filtered[:, channels:2 * channels]
    values = filtered[:, 2 * channels:]
    signal = gate_in * values
    padded_len = 2 * row_count
    spectrum = jnp.fft.rfft(signal, n=padded_len, axis=0) * jnp.fft.rfft(long_filter, n=padded_len, axis=0)
    long_part = jnp.fft.irfft(spectrum, n=padded_len, axis=0)[:row_count]
    mixed_out = gate_out * (long_part + skip_gain * signal)
    return mixed_out.astype(jnp.bfloat16)
```

```python
import math

import jax
import jax.numpy as jnp
import numpy as np
from jax import lax
from jax.experimental import pallas as pl
from jax.experimental.pallas import tpu as pltpu
from jax.sharding import PartitionSpec as P

AXES = ("row", "col")
EPSILON = 1e-05
LANES = 128


def transform_tables(blocks, lanes):
    n = blocks * lanes
    k = np.arange(blocks)
    angle_one = 2.0 * np.pi * np.outer(4 * k + 1, np.arange(blocks)) / (4 * blocks)
    angle_twist = 2.0 * np.pi * np.outer(4 * k + 1, np.arange(lanes)) / (4 * n)
    angle_two = 2.0 * np.pi * np.outer(np.arange(lanes), np.arange(lanes)) / lanes
    first = np.concatenate([np.cos(angle_one), -np.sin(angle_one)], axis=0)
    c, s = np.cos(angle_two), np.sin(angle_two)
    second = np.block([[c, -s], [s, c]])
    second_back = np.block([[c, s], [-s, c]])
    first_back = first.T / n
    half = [x.astype(np.float32).astype(jnp.bfloat16) for x in (first, second, second_back, first_back)]
    twist = np.stack([np.cos(angle_twist), np.sin(angle_twist)]).astype(np.float32)
    return half, twist


def project_table(embedding, norm_gain, w_in):
    rows_f32 = embedding.astype(jnp.float32)
    inverse_rms = lax.rsqrt(jnp.mean(rows_f32 * rows_f32, axis=1, keepdims=True) + EPSILON)
    normed = (rows_f32 * inverse_rms * norm_gain.astype(jnp.float32)).astype(jnp.bfloat16)
    return lax.dot_general(
        w_in, normed, (((0,), (1,)), ((), ())), preferred_element_type=jnp.float32
    ).astype(jnp.bfloat16)


def forward_pair(pair, first_ref, cos, sin, second_ref):
    blocks, lanes = cos.shape
    a = jnp.dot(first_ref[...], pair, preferred_element_type=jnp.float32)
    rows = []
    for h in range(2):
        re = a[:blocks, h * lanes : (h + 1) * lanes]
        im = a[blocks:, h * lanes : (h + 1) * lanes]
        rows.append(
            jnp.concatenate([re * cos + im * sin, im * cos - re * sin], axis=1).astype(jnp.bfloat16)
        )
    turned = jnp.concatenate(rows, axis=0)
    return jnp.dot(turned, second_ref[...], preferred_element_type=jnp.float32)


def signal_kernel(
    token_ref, table_ref, taps_ref, first_ref, twist_ref, second_ref,
    gate_ref, signal_ref, spectrum_ref, taps_wide, previous,
):
    vocab = table_ref.shape[1]
    blocks, lanes = token_ref.shape
    rows = table_ref.shape[0]
    width = rows // 3
    tap_count = taps_ref.shape[1]
    for i in range(tap_count):
        taps_wide[i] = jnp.broadcast_to(taps_ref[:, i : i + 1], (rows, lanes))
    previous[...] = jnp.zeros_like(previous)
    lane = lax.broadcasted_iota(jnp.int32, (rows, lanes), 1)

    @pl.loop(0, blocks // 2)
    def _(step):
        ids = token_ref[pl.ds(2 * step, 2), :]
        entry = lax.broadcasted_iota(jnp.int32, (vocab, lanes), 0)
        one_hot = jnp.concatenate(
            [(entry == ids[h : h + 1, :]).astype(jnp.float32).astype(jnp.bfloat16) for h in range(2)], axis=1
        )
        mixed = jnp.dot(table_ref[...], one_hot, preferred_element_type=jnp.float32)
        before = previous[...]
        for h in range(2):
            here = mixed[:, h * lanes : (h + 1) * lanes]
            total = taps_wide[0] * here
            for i in range(1, tap_count):
                joined = jnp.where(lane >= lanes - i, before, here)
                total = total + taps_wide[i] * pltpu.roll(joined, i, 1)
            begin = pl.multiple_of((2 * step + h) * width, width)
            gate_ref[pl.ds(begin, width), :] = total[:width]
            signal_ref[pl.ds(begin, width), :] = total[width : 2 * width] * total[2 * width :]
            before = here
        previous[...] = before

    cos = twist_ref[0]
    sin = twist_ref[1]

    for q in range(width // 2):
        pair = jnp.concatenate(
            [signal_ref[pl.ds(2 * q + h, blocks, stride=width), :] for h in range(2)], axis=1
        ).astype(jnp.bfloat16)
        z = forward_pair(pair, first_ref, cos, sin, second_ref)
        spectrum_ref[pl.ds(2 * q * blocks, 2 * blocks), :] = z.astype(jnp.bfloat16)


def long_kernel(
    filter_ref, spectrum_ref, gate_ref, signal_ref, skip_ref, first_ref, twist_ref, second_ref,
    second_back_ref, first_back_ref, out_ref, filter_f32, long_part,
):
    blocks, lanes = twist_ref.shape[1:]
    width = skip_ref.shape[0]
    filter_f32[...] = filter_ref[...].astype(jnp.float32)
    cos = twist_ref[0]
    sin = twist_ref[1]

    for q in range(width // 2):
        pair = jnp.concatenate(
            [filter_f32[pl.ds(2 * q + h, blocks, stride=width), :] for h in range(2)], axis=1
        ).astype(jnp.bfloat16)
        f = forward_pair(pair, first_ref, cos, sin, second_ref)
        s = spectrum_ref[pl.ds(2 * q * blocks, 2 * blocks), :].astype(jnp.float32)
        f_re, f_im, s_re, s_im = f[:, :lanes], f[:, lanes:], s[:, :lanes], s[:, lanes:]
        product = jnp.concatenate(
            [f_re * s_re - f_im * s_im, f_re * s_im + f_im * s_re], axis=1
        ).astype(jnp.bfloat16)
        back = jnp.dot(product, second_back_ref[...], preferred_element_type=jnp.float32)
        columns = []
        for h in range(2):
            re = back[h * blocks : (h + 1) * blocks, :lanes]
            im = back[h * blocks : (h + 1) * blocks, lanes:]
            columns.append(jnp.concatenate([re * cos - im * sin, im * cos + re * sin], axis=0).astype(jnp.bfloat16))
        y = jnp.dot(
            first_back_ref[...], jnp.concatenate(columns, axis=1), preferred_element_type=jnp.float32
        )
        for h in range(2):
            long_part[pl.ds(2 * q + h, blocks, stride=width), :] = y[:, h * lanes : (h + 1) * lanes]

    skip = jnp.broadcast_to(skip_ref[...], (width, lanes))

    @pl.loop(0, blocks)
    def _(b):
        at = pl.ds(pl.multiple_of(b * width, width), width)
        out_ref[at, :] = (gate_ref[at, :] * (long_part[at, :] + skip * signal_ref[at, :])).astype(jnp.bfloat16)


def local(token_ids, embedding, norm_gain, w_in, short_taps, long_filter, skip_gain):
    devices = lax.axis_size(AXES)
    me = lax.axis_index(AXES)
    positions, channels = long_filter.shape
    width = channels // devices
    vocab = embedding.shape[0]
    tap_count = short_taps.shape[0]
    blocks = devices * positions // LANES
    (first, second, second_back, first_back), twist = transform_tables(blocks, LANES)

    sent_filter = long_filter.astype(jnp.bfloat16).T.reshape(devices, width, positions)
    filter_all = lax.all_to_all(sent_filter, AXES, split_axis=0, concat_axis=0, tiled=True)
    tokens_all = lax.all_to_all(
        jnp.broadcast_to(token_ids[None], (devices, positions)), AXES, split_axis=0, concat_axis=0, tiled=True
    )

    own = project_table(embedding, norm_gain, w_in)
    chunks = jnp.stack(
        [
            lax.ppermute(own[j * width : (j + 1) * width], AXES, [(d, (3 * d + j) % devices) for d in range(devices)])
            for j in range(3)
        ]
    )
    table = jnp.concatenate(
        [lax.dynamic_index_in_dim(chunks, (me + g * devices) % 3, 0, keepdims=False) for g in range(3)], axis=0
    )
    taps = lax.dynamic_index_in_dim(short_taps.reshape(tap_count, 3, devices, width), me, 2, keepdims=False)
    taps = taps.reshape(tap_count, 3 * width).T
    skip = lax.dynamic_slice_in_dim(skip_gain, me * width, width, 0)[:, None]

    rows = blocks * width
    gate, signal, spectrum = pl.pallas_call(
        signal_kernel,
        out_shape=(
            jax.ShapeDtypeStruct((rows, LANES), jnp.float32),
            jax.ShapeDtypeStruct((rows, LANES), jnp.float32),
            jax.ShapeDtypeStruct((width * blocks, 2 * LANES), jnp.bfloat16),
        ),
        scratch_shapes=[
            pltpu.VMEM((tap_count, 3 * width, LANES), jnp.float32),
            pltpu.VMEM((3 * width, LANES), jnp.float32),
        ],
        compiler_params=pltpu.CompilerParams(vmem_limit_bytes=32 * 1024 * 1024),
        name="signal_spectrum",
    )(tokens_all.reshape(blocks, LANES), table, taps, first, twist, second)
    out = pl.pallas_call(
        long_kernel,
        out_shape=jax.ShapeDtypeStruct((rows, LANES), jnp.bfloat16),
        scratch_shapes=[
            pltpu.VMEM((rows, LANES), jnp.float32),
            pltpu.VMEM((rows, LANES), jnp.float32),
        ],
        compiler_params=pltpu.CompilerParams(vmem_limit_bytes=32 * 1024 * 1024),
        name="long_convolution",
    )(filter_all.reshape(rows, LANES), spectrum, gate, signal, skip, first, twist, second, second_back, first_back)

    sent_out = out.reshape(devices, width, positions)
    received = lax.all_to_all(sent_out, AXES, split_axis=0, concat_axis=0, tiled=True)
    return received.reshape(channels, positions).T


def solution(mesh):
    in_specs = (
        P(AXES),
        P(),
        P(),
        P(None, AXES),
        P(),
        P(AXES, None),
        P(),
    )
    out_specs = P(AXES, None)
    return jax.shard_map(local, mesh=mesh, in_specs=in_specs, out_specs=out_specs, check_vma=False)
```

```python
import functools

import jax
import jax.numpy as jnp
import numpy as np
from jax import lax
from jax.experimental import pallas as pl
from jax.experimental.pallas import tpu as pltpu
from jax.sharding import PartitionSpec as P

AXES = ("row", "col")
EPSILON = 1e-05
LANES = 128
AT_ONCE = 32
TOGETHER = 8
F32 = jnp.float32
BF16 = jnp.bfloat16


def transform_tables(blocks, lanes):
    n = blocks * lanes
    k = np.arange(blocks)
    angle_one = 2.0 * np.pi * np.outer(4 * k + 1, np.arange(blocks)) / (4 * blocks)
    angle_twist = 2.0 * np.pi * np.outer(4 * k + 1, np.arange(lanes)) / (4 * n)
    angle_two = 2.0 * np.pi * np.outer(np.arange(lanes), np.arange(lanes)) / lanes
    first = np.concatenate([np.cos(angle_one), -np.sin(angle_one)], axis=0)
    c, s = np.cos(angle_two), np.sin(angle_two)
    second = np.block([[c, -s], [s, c]])
    second_back = np.block([[c, s], [-s, c]])
    first_back = first.T / n
    half = [x.astype(np.float32).astype(jnp.bfloat16) for x in (first, second, second_back, first_back)]
    twist = np.stack([np.cos(angle_twist), np.sin(angle_twist)]).astype(np.float32)
    return half, twist


def dot(a, b):
    return jnp.dot(a, b, preferred_element_type=F32)


def project_table(embedding, norm_gain, w_in):
    rows_f32 = embedding.astype(F32)
    inverse_rms = lax.rsqrt(jnp.mean(rows_f32 * rows_f32, axis=1, keepdims=True) + EPSILON)
    normed = (rows_f32 * inverse_rms * norm_gain.astype(F32)).astype(BF16)
    return lax.dot_general(w_in, normed, (((0,), (1,)), ((), ())), preferred_element_type=F32).astype(BF16)


def pack_kernel(filter_ref, code_ref, out_ref):
    count, rows, positions = out_ref.shape
    width = rows - 1
    turned = filter_ref[...].T
    for d in range(count):
        out_ref[d] = jnp.concatenate([turned[d * width : (d + 1) * width], code_ref[...]], axis=0).astype(BF16)


def conv_kernel(
    me_ref, arrived_ref, chunk0_ref, chunk1_ref, chunk2_ref, taps_ref, skip_ref, first_ref, twist_ref,
    second_ref, second_back_ref, first_back_ref,
    out_ref, filter_s, gate, signal, mixed, codes_s, long_s, chunks, small, *, pitch,
):
    blocks, rows_in, lanes = arrived_ref.shape
    width = rows_in - 1
    rows = 3 * width
    vocab = chunk0_ref.shape[1]
    half = vocab // 2
    tap_count = taps_ref.shape[0]
    channels = taps_ref.shape[1] // 3
    me = me_ref[0]

    share = lanes // width
    small[...] = jnp.zeros_like(small)
    for g in range(3):
        begin = pl.multiple_of(g * channels + me // share * lanes, lanes)
        small[8 * g : 8 * g + tap_count, :] = taps_ref[:, pl.ds(begin, lanes)]
    small[7:8, :] = skip_ref[pl.ds(me // share, 1), :]
    small[...] = small[...].T
    columns = small[pl.ds(pl.multiple_of(me % share * width, 8), width), :]

    chunks[0] = chunk0_ref[...]
    chunks[1] = chunk1_ref[...]
    chunks[2] = chunk2_ref[...]
    parts = [chunks[(me + g * blocks) % 3] for g in range(3)]
    folded = jnp.concatenate([x[:, :half] for x in parts] + [x[:, half:] for x in parts], axis=0)

    def cast_step(b, carry):
        got = arrived_ref[b].astype(F32)
        filter_s[pl.ds(b * pitch, width), :] = got[:width]
        codes_s[pl.ds(b, 1), :] = got[width:]
        return carry

    lax.fori_loop(0, blocks, cast_step, 0, unroll=8)
    codes_s[...] = codes_s[...].T

    def look_up(step, carry):
        found = []
        hots = []
        entry = lax.broadcasted_iota(jnp.int32, (half, blocks), 0).astype(F32) + 1.0
        for h in range(AT_ONCE):
            code = codes_s[pl.ds(AT_ONCE * step + h, 1), :]
            found.append(code)
            hots.append((entry == jnp.abs(code)).astype(F32).astype(BF16))
        both = dot(folded, jnp.concatenate(hots, axis=1))
        for h in range(AT_ONCE):
            here = both[:, h * blocks : (h + 1) * blocks]
            begin = pl.multiple_of((AT_ONCE * step + h + 8) * rows, 8)
            mixed[pl.ds(begin, rows), :] = jnp.where(found[h] < 0.0, here[rows:], here[:rows])
        return carry

    lax.fori_loop(0, lanes // AT_ONCE, look_up, 0)
    block = lax.broadcasted_iota(jnp.int32, (rows, blocks), 1)
    for i in range(1, tap_count):
        last = mixed[(lanes + 8 - i) * rows : (lanes + 9 - i) * rows, :]
        mixed[(8 - i) * rows : (9 - i) * rows, :] = jnp.where(block == 0, 0.0, pltpu.roll(last, 1, 1))

    for c in range(0, width, 8):
        taps = [
            [jnp.broadcast_to(columns[c : c + 8, 8 * g + i : 8 * g + i + 1], (8, blocks)) for i in range(tap_count)]
            for g in range(3)
        ]

        def at(p, g):
            return mixed[pl.ds(pl.multiple_of((p + 8) * rows + g * width + c, 8), 8), :]

        def filter_step(p, window):
            later = []
            total = []
            for g in range(3):
                here = at(p, g)
                value = taps[g][0] * here
                for i in range(1, tap_count):
                    value = value + taps[g][i] * window[g][i - 1]
                total.append(value)
                later.append((here,) + window[g][:-1])
            gate[pl.ds(p * pitch + c, 8), :] = total[0]
            signal[pl.ds(p * pitch + c, 8), :] = total[1] * total[2]
            return tuple(later)

        before = tuple(tuple(at(-i, g) for i in range(1, tap_count)) for g in range(3))
        lax.fori_loop(0, lanes, filter_step, before, unroll=8)

    cos = twist_ref[0]
    sin = twist_ref[1]

    def channel(ref, c):
        return ref[pl.ds(c, ref.shape[0] // pitch, stride=pitch), :]

    for begin in range(0, width, TOGETHER):
        own = range(begin, begin + TOGETHER)
        signals = [channel(signal, c).T for c in own]
        series = [x for c, s in zip(own, signals) for x in (s, channel(filter_s, c))]
        turned = []
        for j in range(0, 2 * TOGETHER, 2):
            a = dot(first_ref[...], jnp.concatenate(series[j : j + 2], axis=1).astype(BF16))
            for h in range(2):
                re = a[:blocks, h * lanes : (h + 1) * lanes]
                im = a[blocks:, h * lanes : (h + 1) * lanes]
                turned.append(jnp.concatenate([re * cos + im * sin, im * cos - re * sin], axis=1).astype(BF16))
        z = dot(jnp.concatenate(turned, axis=0), second_ref[...])
        products = []
        for h in range(TOGETHER):
            s = z[2 * h * blocks : (2 * h + 1) * blocks]
            f = z[(2 * h + 1) * blocks : (2 * h + 2) * blocks]
            s_re, s_im, f_re, f_im = s[:, :lanes], s[:, lanes:], f[:, :lanes], f[:, lanes:]
            products.append(
                jnp.concatenate([f_re * s_re - f_im * s_im, f_re * s_im + f_im * s_re], axis=1).astype(BF16)
            )
        back = dot(jnp.concatenate(products, axis=0), second_back_ref[...])
        unturned = []
        for h in range(TOGETHER):
            re = back[h * blocks : (h + 1) * blocks, :lanes]
            im = back[h * blocks : (h + 1) * blocks, lanes:]
            unturned.append(jnp.concatenate([re * cos - im * sin, im * cos + re * sin], axis=0).astype(BF16))
        for j in range(0, TOGETHER, 2):
            y = dot(first_back_ref[...], jnp.concatenate(unturned[j : j + 2], axis=1))
            for h in range(2):
                c = begin + j + h
                inner = y[:, h * lanes : (h + 1) * lanes] + columns[c : c + 1, 7:8] * signals[j + h]
                long_s[pl.ds(c, blocks, stride=pitch), :] = channel(gate, c).T * inner

    def round_step(b, carry):
        out_ref[pl.ds(pl.multiple_of(b * width, width), width), :] = long_s[pl.ds(b * pitch, width), :].astype(BF16)
        return carry

    lax.fori_loop(0, blocks, round_step, 0, unroll=8)


def local(token_ids, embedding, norm_gain, w_in, short_taps, long_filter, skip_gain):
    devices = lax.axis_size(AXES)
    me = lax.axis_index(AXES)
    positions, channels = long_filter.shape
    width = channels // devices
    vocab = embedding.shape[0]
    half = vocab // 2
    tap_count = short_taps.shape[0]
    blocks = devices
    rows = 3 * width
    (first, second, second_back, first_back), twist = transform_tables(blocks, positions)

    code = jnp.where(token_ids < half, token_ids + 1, half - 1 - token_ids).astype(F32)[None]
    steps = 8
    sent = pl.pallas_call(
        pack_kernel,
        grid=(steps,),
        in_specs=[
            pl.BlockSpec((positions, channels // steps), lambda i: (0, i)),
            pl.BlockSpec((1, positions), lambda i: (0, 0)),
        ],
        out_specs=pl.BlockSpec((devices // steps, width + 1, positions), lambda i: (i, 0, 0)),
        out_shape=jax.ShapeDtypeStruct((devices, width + 1, positions), BF16),
        name="pack",
    )(long_filter, code)
    arrived = lax.all_to_all(sent, AXES, split_axis=0, concat_axis=0, tiled=True)

    own = project_table(embedding, norm_gain, w_in)
    chunks = [
        lax.ppermute(own[j * width : (j + 1) * width], AXES, [(d, (3 * d + j) % devices) for d in range(devices)])
        for j in range(3)
    ]

    pitch = width + 1
    vmem = pl.BlockSpec(memory_space=pltpu.VMEM)
    out = pl.pallas_call(
        functools.partial(conv_kernel, pitch=pitch),
        in_specs=[pl.BlockSpec(memory_space=pltpu.SMEM)] + [vmem] * 11,
        out_specs=vmem,
        out_shape=jax.ShapeDtypeStruct((blocks * width, positions), BF16),
        scratch_shapes=[
            pltpu.VMEM((blocks * pitch, positions), F32),
            pltpu.VMEM((positions * pitch, blocks), F32),
            pltpu.VMEM((positions * pitch, blocks), F32),
            pltpu.VMEM(((positions + 8) * rows, blocks), F32),
            pltpu.VMEM((blocks, positions), F32),
            pltpu.VMEM((blocks * pitch, positions), F32),
            pltpu.VMEM((3, width, vocab), BF16),
            pltpu.VMEM((positions, positions), F32),
        ],
        compiler_params=pltpu.CompilerParams(vmem_limit_bytes=48 * 1024 * 1024),
        name="convolution",
    )(
        me[None].astype(jnp.int32), arrived, *chunks, short_taps, skip_gain.reshape(channels // LANES, LANES),
        first, twist, second, second_back, first_back,
    )

    received = lax.all_to_all(
        out.reshape(devices, width, positions), AXES, split_axis=0, concat_axis=0, tiled=True
    )
    return received.reshape(channels, positions).T


def solution(mesh):
    in_specs = (
        P(AXES),
        P(),
        P(),
        P(None, AXES),
        P(),
        P(AXES, None),
        P(),
    )
    out_specs = P(AXES, None)
    return jax.shard_map(local, mesh=mesh, in_specs=in_specs, out_specs=out_specs, check_vma=False)
```

```python
import functools

import jax
import jax.numpy as jnp
import numpy as np
from jax import lax
from jax.experimental import pallas as pl
from jax.experimental.pallas import tpu as pltpu
from jax.sharding import PartitionSpec as P

AXES = ("row", "col")
EPSILON = 1e-05
LANES = 128
AT_ONCE = 32
TOGETHER = 8
F32 = jnp.float32
BF16 = jnp.bfloat16


def transform_tables(blocks, lanes):
    n = blocks * lanes
    k = np.arange(blocks)
    angle_one = 2.0 * np.pi * np.outer(4 * k + 1, np.arange(blocks)) / (4 * blocks)
    angle_twist = 2.0 * np.pi * np.outer(4 * k + 1, np.arange(lanes)) / (4 * n)
    angle_two = 2.0 * np.pi * np.outer(np.arange(lanes), np.arange(lanes)) / lanes
    first = np.concatenate([np.cos(angle_one), -np.sin(angle_one)], axis=0)
    c, s = np.cos(angle_two), np.sin(angle_two)
    second = np.block([[c, -s], [s, c]])
    second_back = np.block([[c, s], [-s, c]])
    first_back = first.T / n
    pieces = [second, second_back, first_back, np.concatenate([first[:blocks], first[blocks:]], axis=1)]
    matrices = np.concatenate(pieces, axis=0).astype(np.float32).astype(jnp.bfloat16)
    twist = np.stack([np.cos(angle_twist), np.sin(angle_twist)]).astype(np.float32)
    return matrices, twist


def dot(a, b):
    return jnp.dot(a, b, preferred_element_type=F32)


def table_kernel(embedding_ref, gain_ref, w_ref, out0_ref, out1_ref, out2_ref, scaled, *, step):
    depth = embedding_ref.shape[1]
    width = out0_ref.shape[0]
    for k in range(0, depth, 1024):
        at = slice(k, k + 1024)
        scaled[:, at] = (w_ref[:, at].astype(F32) * gain_ref[:, at].astype(F32)).astype(BF16)
    for r in range(0, embedding_ref.shape[0], step):
        product = lax.dot_general(
            scaled[...], embedding_ref[r : r + step, :], (((1,), (1,)), ((), ())), preferred_element_type=F32
        )
        squares = jnp.zeros((step, LANES), F32)
        for k in range(0, depth, LANES):
            x = embedding_ref[r : r + step, k : k + LANES].astype(F32)
            squares = squares + x * x
        inverse_rms = lax.rsqrt(jnp.sum(squares.T, axis=0, keepdims=True) * (1.0 / depth) + EPSILON)
        part = (product * inverse_rms).astype(BF16)
        out0_ref[:, r : r + step] = part[:width]
        out1_ref[:, r : r + step] = part[width : 2 * width]
        out2_ref[:, r : r + step] = part[2 * width :]


def pack_kernel(filter_ref, ids_ref, out_ref, *, half):
    count, rows, positions = out_ref.shape
    width = rows - 1
    ids = ids_ref[...]
    code = jnp.where(ids < half, ids + 1, half - 1 - ids).astype(F32).astype(BF16)
    group = LANES // width
    for d in range(0, count, group):
        turned = filter_ref[:, d * width : (d + group) * width].T.astype(BF16)
        for e in range(group):
            out_ref[d + e] = jnp.concatenate([turned[e * width : (e + 1) * width], code], axis=0)


def conv_kernel(
    me_ref, arrived_ref, chunk0_ref, chunk1_ref, chunk2_ref, taps_ref, skip_ref, matrices_ref, twist_ref, out_ref,
    filter_s, gate, signal, mixed, codes_s, long_s, chunks, small, *, pitch,
):
    blocks, rows_in, lanes = arrived_ref.shape
    width = rows_in - 1
    rows = 3 * width
    vocab = chunk0_ref.shape[1]
    half = vocab // 2
    tap_count = taps_ref.shape[0]
    channels = taps_ref.shape[1] // 3
    me = me_ref[0]

    share = lanes // width
    small[...] = jnp.zeros_like(small)
    for g in range(3):
        begin = pl.multiple_of(g * channels + me // share * lanes, lanes)
        small[8 * g : 8 * g + tap_count, :] = taps_ref[:, pl.ds(begin, lanes)]
    small[7:8, :] = skip_ref[pl.ds(me // share, 1), :]
    small[...] = small[...].T
    columns = small[pl.ds(pl.multiple_of(me % share * width, 8), width), :]

    chunks[0] = chunk0_ref[...]
    chunks[1] = chunk1_ref[...]
    chunks[2] = chunk2_ref[...]
    parts = [chunks[(me + g * blocks) % 3] for g in range(3)]
    folded = jnp.concatenate([x[:, :half] for x in parts] + [x[:, half:] for x in parts], axis=0)

    def cast_step(b, carry):
        got = arrived_ref[b].astype(F32)
        filter_s[pl.ds(b * pitch, width), :] = got[:width]
        codes_s[pl.ds(b, 1), :] = got[width:]
        return carry

    lax.fori_loop(0, blocks, cast_step, 0, unroll=8)
    codes_s[...] = codes_s[...].T

    def look_up(step, carry):
        found = []
        hots = []
        entry = lax.broadcasted_iota(jnp.int32, (half, blocks), 0).astype(F32) + 1.0
        for h in range(AT_ONCE):
            code = codes_s[pl.ds(AT_ONCE * step + h, 1), :]
            found.append(code)
            hots.append((entry == jnp.abs(code)).astype(F32).astype(BF16))
        both = dot(folded, jnp.concatenate(hots, axis=1))
        for h in range(AT_ONCE):
            here = both[:, h * blocks : (h + 1) * blocks]
            begin = pl.multiple_of((AT_ONCE * step + h + 8) * rows, 8)
            mixed[pl.ds(begin, rows), :] = jnp.where(found[h] < 0.0, here[rows:], here[:rows])
        return carry

    lax.fori_loop(0, lanes // AT_ONCE, look_up, 0)
    block = lax.broadcasted_iota(jnp.int32, (rows, blocks), 1)
    for i in range(1, tap_count):
        last = mixed[(lanes + 8 - i) * rows : (lanes + 9 - i) * rows, :]
        mixed[(8 - i) * rows : (9 - i) * rows, :] = jnp.where(block == 0, 0.0, pltpu.roll(last, 1, 1))

    for c in range(0, width, 8):
        taps = [
            [jnp.broadcast_to(columns[c : c + 8, 8 * g + i : 8 * g + i + 1], (8, blocks)) for i in range(tap_count)]
            for g in range(3)
        ]

        def at(p, g):
            return mixed[pl.ds(pl.multiple_of((p + 8) * rows + g * width + c, 8), 8), :]

        def filter_step(p, window):
            later = []
            total = []
            for g in range(3):
                here = at(p, g)
                value = taps[g][0] * here
                for i in range(1, tap_count):
                    value = value + taps[g][i] * window[g][i - 1]
                total.append(value)
                later.append((here,) + window[g][:-1])
            gate[pl.ds(p * pitch + c, 8), :] = total[0]
            signal[pl.ds(p * pitch + c, 8), :] = total[1] * total[2]
            return tuple(later)

        before = tuple(tuple(at(-i, g) for i in range(1, tap_count)) for g in range(3))
        lax.fori_loop(0, lanes, filter_step, before, unroll=8)

    cos = twist_ref[0]
    sin = twist_ref[1]
    side = 2 * lanes
    second = matrices_ref[:side, :]
    second_back = matrices_ref[side : 2 * side, :]
    first_back = matrices_ref[2 * side : 2 * side + blocks, :]
    both_first = matrices_ref[2 * side + blocks :, :]
    first = jnp.concatenate([both_first[:, :blocks], both_first[:, blocks:]], axis=0)

    def channel(ref, c):
        return ref[pl.ds(c, ref.shape[0] // pitch, stride=pitch), :]

    for begin in range(0, width, TOGETHER):
        own = range(begin, begin + TOGETHER)
        signals = [channel(signal, c).T for c in own]
        series = [x for c, s in zip(own, signals) for x in (s, channel(filter_s, c))]
        turned = []
        for j in range(0, 2 * TOGETHER, 2):
            a = dot(first, jnp.concatenate(series[j : j + 2], axis=1).astype(BF16))
            for h in range(2):
                re = a[:blocks, h * lanes : (h + 1) * lanes]
                im = a[blocks:, h * lanes : (h + 1) * lanes]
                turned.append(jnp.concatenate([re * cos + im * sin, im * cos - re * sin], axis=1).astype(BF16))
        z = dot(jnp.concatenate(turned, axis=0), second)
        products = []
        for h in range(TOGETHER):
            s = z[2 * h * blocks : (2 * h + 1) * blocks]
            f = z[(2 * h + 1) * blocks : (2 * h + 2) * blocks]
            s_re, s_im, f_re, f_im = s[:, :lanes], s[:, lanes:], f[:, :lanes], f[:, lanes:]
            products.append(
                jnp.concatenate([f_re * s_re - f_im * s_im, f_re * s_im + f_im * s_re], axis=1).astype(BF16)
            )
        back = dot(jnp.concatenate(products, axis=0), second_back)
        unturned = []
        for h in range(TOGETHER):
            re = back[h * blocks : (h + 1) * blocks, :lanes]
            im = back[h * blocks : (h + 1) * blocks, lanes:]
            unturned.append(jnp.concatenate([re * cos - im * sin, im * cos + re * sin], axis=0).astype(BF16))
        for j in range(0, TOGETHER, 2):
            y = dot(first_back, jnp.concatenate(unturned[j : j + 2], axis=1))
            for h in range(2):
                c = begin + j + h
                inner = y[:, h * lanes : (h + 1) * lanes] + columns[c : c + 1, 7:8] * signals[j + h]
                long_s[pl.ds(c, blocks, stride=pitch), :] = channel(gate, c).T * inner

    def round_step(b, carry):
        out_ref[pl.ds(pl.multiple_of(b * width, width), width), :] = long_s[pl.ds(b * pitch, width), :].astype(BF16)
        return carry

    lax.fori_loop(0, blocks, round_step, 0, unroll=8)


def conv_call(me, arrived, chunk0, chunk1, chunk2, short_taps, skip_gain, matrices, twist):
    blocks, rows_in, positions = arrived.shape
    width, vocab = chunk0.shape
    rows = 3 * width
    pitch = width + 1
    vmem = pl.BlockSpec(memory_space=pltpu.VMEM)
    return pl.pallas_call(
        functools.partial(conv_kernel, pitch=pitch),
        in_specs=[pl.BlockSpec(memory_space=pltpu.SMEM)] + [vmem] * 8,
        out_specs=vmem,
        out_shape=jax.ShapeDtypeStruct((blocks * width, positions), BF16),
        scratch_shapes=[
            pltpu.VMEM((blocks * pitch, positions), F32),
            pltpu.VMEM((positions * pitch, blocks), F32),
            pltpu.VMEM((positions * pitch, blocks), F32),
            pltpu.VMEM(((positions + 8) * rows, blocks), F32),
            pltpu.VMEM((blocks, positions), F32),
            pltpu.VMEM((blocks * pitch, positions), F32),
            pltpu.VMEM((3, width, vocab), BF16),
            pltpu.VMEM((positions, positions), F32),
        ],
        compiler_params=pltpu.CompilerParams(vmem_limit_bytes=32 * 1024 * 1024),
        name="convolution",
    )(me, arrived, chunk0, chunk1, chunk2, short_taps, skip_gain, matrices, twist)


def local(token_ids, embedding, norm_gain, w_in, short_taps, long_filter, skip_gain):
    devices = lax.axis_size(AXES)
    me = lax.axis_index(AXES)
    positions, channels = long_filter.shape
    width = channels // devices
    vocab = embedding.shape[0]
    half = vocab // 2
    blocks = devices
    rows = 3 * width
    matrices, twist = transform_tables(blocks, positions)

    vmem = pl.BlockSpec(memory_space=pltpu.VMEM)
    sent = pl.pallas_call(
        functools.partial(pack_kernel, half=half),
        in_specs=[vmem, vmem],
        out_specs=vmem,
        out_shape=jax.ShapeDtypeStruct((devices, width + 1, positions), BF16),
        compiler_params=pltpu.CompilerParams(vmem_limit_bytes=8 * 1024 * 1024),
        name="pack",
    )(long_filter, token_ids[None])
    arrived = lax.all_to_all(sent, AXES, split_axis=0, concat_axis=0, tiled=True)

    own = pl.pallas_call(
        functools.partial(table_kernel, step=LANES),
        in_specs=[vmem] * 3,
        out_specs=[vmem] * 3,
        out_shape=[jax.ShapeDtypeStruct((width, vocab), BF16)] * 3,
        scratch_shapes=[pltpu.VMEM((rows, embedding.shape[1]), BF16)],
        compiler_params=pltpu.CompilerParams(vmem_limit_bytes=20 * 1024 * 1024),
        name="table",
    )(embedding, norm_gain[None], w_in.T)
    chunks = [
        lax.ppermute(own[j], AXES, [(d, (3 * d + j) % devices) for d in range(devices)]) for j in range(3)
    ]

    out = conv_call(me[None].astype(jnp.int32), arrived, *chunks, short_taps, skip_gain.reshape(channels // LANES, LANES), matrices, twist)
    received = lax.all_to_all(
        out.reshape(devices, width, positions), AXES, split_axis=0, concat_axis=0, tiled=True
    )
    return received.reshape(channels, positions).T


def solution(mesh):
    in_specs = (
        P(AXES),
        P(),
        P(),
        P(None, AXES),
        P(),
        P(AXES, None),
        P(),
    )
    out_specs = P(AXES, None)
    return jax.shard_map(local, mesh=mesh, in_specs=in_specs, out_specs=out_specs, check_vma=False)
```

```python
import functools

import jax
import jax.numpy as jnp
import numpy as np
from jax import lax
from jax.experimental import pallas as pl
from jax.experimental.pallas import tpu as pltpu
from jax.sharding import PartitionSpec as P

AXES = ("row", "col")
EPSILON = 1e-05
LANES = 128
AT_ONCE = 32
PACK_VMEM = 62
TABLE_VMEM = 20
TOGETHER = 8
F32 = jnp.float32
BF16 = jnp.bfloat16


def transform_tables(blocks, lanes):
    n = blocks * lanes
    k = np.arange(blocks)
    angle_one = 2.0 * np.pi * np.outer(4 * k + 1, np.arange(blocks)) / (4 * blocks)
    angle_twist = 2.0 * np.pi * np.outer(4 * k + 1, np.arange(lanes)) / (4 * n)
    angle_two = 2.0 * np.pi * np.outer(np.arange(lanes), np.arange(lanes)) / lanes
    one = np.concatenate([np.cos(angle_one), -np.sin(angle_one)], axis=1)
    two = np.concatenate([np.cos(angle_two), np.sin(angle_two)], axis=1)
    back = np.concatenate([np.cos(angle_one).T, -np.sin(angle_one).T], axis=1) / n
    rounded = np.concatenate([one, two, back], axis=0).astype(np.float32).astype(jnp.bfloat16).astype(np.float32)
    twist = np.concatenate([np.cos(angle_twist), np.sin(angle_twist)], axis=1).astype(np.float32)
    return np.concatenate([twist, rounded], axis=0)


def dot(a, b):
    return jnp.dot(a, b, preferred_element_type=F32)


def table_kernel(
    me_ref, embedding_ref, gain_ref, w_ref, taps_hbm, skip_hbm, out0_ref, out1_ref, out2_ref, columns_ref,
    normed, gain_wide, small, small_arrived,
):
    vocab, depth = embedding_ref.shape
    width = out0_ref.shape[0]
    tap_count = taps_hbm.shape[0]
    channels = taps_hbm.shape[1] // 3
    share = LANES // width
    me = me_ref[0]
    few = [pltpu.make_async_copy(skip_hbm.at[pl.ds(me // share, 1), :], small.at[pl.ds(24, 1), :], small_arrived.at[3])]
    for g in range(3):
        at = pl.ds(pl.multiple_of(g * channels + me // share * LANES, LANES), LANES)
        few.append(
            pltpu.make_async_copy(taps_hbm.at[:, at], small.at[pl.ds(8 * g, tap_count), :], small_arrived.at[g])
        )
    for copy in few:
        copy.start()
    gain_wide[...] = jnp.broadcast_to(gain_ref[...].astype(F32), gain_wide.shape)
    for copy in few:
        copy.wait()
    small[...] = small[...].T
    columns_ref[...] = small[pl.ds(pl.multiple_of(me % share * width, 8), width), :]

    @pl.loop(0, vocab // LANES)
    def _(part):
        begin = pl.multiple_of(part * LANES, LANES)

        def norm_step(i, carry):
            x = embedding_ref[pl.ds(pl.multiple_of(begin + i * 16, 16), 16), :].astype(F32)
            inverse_rms = lax.rsqrt(jnp.mean(x * x, axis=1, keepdims=True) + EPSILON)
            gain = jnp.concatenate([gain_wide[...]] * 2, axis=0)
            normed[pl.ds(pl.multiple_of(i * 16, 16), 16), :] = (x * inverse_rms * gain).astype(BF16)
            return carry

        lax.fori_loop(0, LANES // 16, norm_step, 0, unroll=8)
        product = lax.dot_general(
            w_ref[...], normed[...], (((1,), (1,)), ((), ())), preferred_element_type=F32
        ).astype(BF16)
        for j, out_ref in enumerate((out0_ref, out1_ref, out2_ref)):
            out_ref[:, pl.ds(begin, LANES)] = product[j * width : (j + 1) * width]


def pack_kernel(filter_hbm, ids_hbm, out_ref, filter_ref, ids_ref, arrived, *, half):
    count, rows, positions = out_ref.shape
    width = rows - 1
    group = LANES // width
    part = filter_hbm.shape[1] // 4
    copies = [pltpu.make_async_copy(ids_hbm, ids_ref, arrived.at[4])]
    for k in range(4):
        at = pl.ds(k * part, part)
        copies.append(pltpu.make_async_copy(filter_hbm.at[:, at], filter_ref.at[:, at], arrived.at[k]))
    for copy in copies:
        copy.start()
    copies[0].wait()
    ids = ids_ref[...]
    code = jnp.where(ids < half, ids + 1, half - 1 - ids).astype(F32).astype(BF16)
    inverse = pow(3, -1, count)
    for q in range(0, count, group):
        if q * width % part == 0:
            copies[1 + q * width // part].wait()
        turned = filter_ref[:, q * width : (q + group) * width].T.astype(BF16)
        for e in range(group):
            out_ref[(q + e) * inverse % count] = jnp.concatenate(
                [turned[e * width : (e + 1) * width], code], axis=0
            )


def unpack_kernel(received_ref, out_ref):
    count, width, positions = received_ref.shape
    inverse = pow(3, -1, count)
    group = LANES // width
    for q in range(0, count, group):
        rows = [received_ref[(q + e) * inverse % count].astype(F32) for e in range(group)]
        out_ref[:, q * width : (q + group) * width] = jnp.concatenate(rows, axis=0).T.astype(BF16)


def matrices(constants_ref):
    lanes = LANES
    blocks = (constants_ref.shape[0] - lanes) // 3
    cos = constants_ref[:blocks, :lanes]
    sin = constants_ref[:blocks, lanes:]
    one = constants_ref[blocks : 2 * blocks, :].astype(BF16)
    first = jnp.concatenate([one[:, :blocks], one[:, blocks:]], axis=0)
    two = constants_ref[2 * blocks : 2 * blocks + lanes, :]
    real, imaginary = two[:, :lanes].astype(BF16), two[:, lanes:].astype(BF16)
    minus = (-two[:, lanes:]).astype(BF16)
    second = jnp.concatenate(
        [jnp.concatenate([real, minus], axis=1), jnp.concatenate([imaginary, real], axis=1)], axis=0
    )
    second_back = jnp.concatenate(
        [jnp.concatenate([real, imaginary], axis=1), jnp.concatenate([minus, real], axis=1)], axis=0
    )
    first_back = constants_ref[2 * blocks + lanes :, :].astype(BF16)
    return cos, sin, first, second, second_back, first_back


def channel(ref, c, pitch):
    return ref[pl.ds(c, ref.shape[0] // pitch, stride=pitch), :]


def forward(series, cos, sin, first, second):
    blocks, lanes = cos.shape
    turned = []
    for j in range(0, len(series), 2):
        a = dot(first, jnp.concatenate(series[j : j + 2], axis=1).astype(BF16))
        for h in range(2):
            re = a[:blocks, h * lanes : (h + 1) * lanes]
            im = a[blocks:, h * lanes : (h + 1) * lanes]
            turned.append(jnp.concatenate([re * cos + im * sin, im * cos - re * sin], axis=1).astype(BF16))
    return dot(jnp.concatenate(turned, axis=0), second)


def filter_kernel(arrived_ref, constants_ref, spectrum_ref, codes_ref, filter_s, *, pitch):
    blocks, rows_in, lanes = arrived_ref.shape
    width = rows_in - 1

    def cast_step(b, carry):
        got = arrived_ref[b].astype(F32)
        filter_s[pl.ds(b * pitch, width), :] = got[:width]
        codes_ref[pl.ds(b, 1), :] = got[width:]
        return carry

    lax.fori_loop(0, blocks, cast_step, 0, unroll=8)
    codes_ref[...] = codes_ref[...].T
    cos, sin, first, second, _, _ = matrices(constants_ref)
    for c in range(0, width, TOGETHER):
        z = forward([channel(filter_s, c + h, pitch) for h in range(TOGETHER)], cos, sin, first, second)
        spectrum_ref[c * blocks : (c + TOGETHER) * blocks, :] = z.astype(BF16)


def conv_kernel(
    me_ref, spectrum_ref, codes_s, chunk0_ref, chunk1_ref, chunk2_ref, columns_ref, constants_ref, out_ref,
    gate, signal, mixed, long_s, chunks, *, tap_count, pitch,
):
    blocks, lanes = codes_s.shape[::-1]
    width = chunk0_ref.shape[0]
    rows = 3 * width
    vocab = chunk0_ref.shape[1]
    half = vocab // 2
    me = me_ref[0]
    columns = columns_ref[...]

    chunks[0] = chunk0_ref[...]
    chunks[1] = chunk1_ref[...]
    chunks[2] = chunk2_ref[...]
    parts = [chunks[(me + g * blocks) % 3] for g in range(3)]
    folded = jnp.concatenate([x[:, :half] for x in parts] + [x[:, half:] for x in parts], axis=0)

    def look_up(step, carry):
        found = []
        hots = []
        entry = lax.broadcasted_iota(jnp.int32, (half, blocks), 0).astype(F32) + 1.0
        for h in range(AT_ONCE):
            code = codes_s[pl.ds(AT_ONCE * step + h, 1), :]
            found.append(code)
            hots.append((entry == jnp.abs(code)).astype(F32).astype(BF16))
        both = dot(folded, jnp.concatenate(hots, axis=1))
        for h in range(AT_ONCE):
            here = both[:, h * blocks : (h + 1) * blocks]
            begin = pl.multiple_of((AT_ONCE * step + h + 8) * rows, 8)
            mixed[pl.ds(begin, rows), :] = jnp.where(found[h] < 0.0, here[rows:], here[:rows])
        return carry

    lax.fori_loop(0, lanes // AT_ONCE, look_up, 0)
    block = lax.broadcasted_iota(jnp.int32, (rows, blocks), 1)
    for i in range(1, tap_count):
        last = mixed[(lanes + 8 - i) * rows : (lanes + 9 - i) * rows, :]
        mixed[(8 - i) * rows : (9 - i) * rows, :] = jnp.where(block == 0, 0.0, pltpu.roll(last, 1, 1))

    for c in range(0, width, 8):
        taps = [
            [jnp.broadcast_to(columns[c : c + 8, 8 * g + i : 8 * g + i + 1], (8, blocks)) for i in range(tap_count)]
            for g in range(3)
        ]

        def at(p, g):
            return mixed[pl.ds(pl.multiple_of((p + 8) * rows + g * width + c, 8), 8), :]

        def filter_step(p, window):
            later = []
            total = []
            for g in range(3):
                here = at(p, g)
                value = taps[g][0] * here
                for i in range(1, tap_count):
                    value = value + taps[g][i] * window[g][i - 1]
                total.append(value)
                later.append((here,) + window[g][:-1])
            gate[pl.ds(p * pitch + c, 8), :] = total[0]
            signal[pl.ds(p * pitch + c, 8), :] = total[1] * total[2]
            return tuple(later)

        before = tuple(tuple(at(-i, g) for i in range(1, tap_count)) for g in range(3))
        lax.fori_loop(0, lanes, filter_step, before, unroll=8)

    cos, sin, first, second, second_back, first_back = matrices(constants_ref)

    for begin in range(0, width, TOGETHER):
        signals = [channel(signal, begin + h, pitch).T for h in range(TOGETHER)]
        z = forward(signals, cos, sin, first, second)
        products = []
        for h in range(TOGETHER):
            s = z[h * blocks : (h + 1) * blocks]
            f = spectrum_ref[(begin + h) * blocks : (begin + h + 1) * blocks, :].astype(F32)
            s_re, s_im, f_re, f_im = s[:, :lanes], s[:, lanes:], f[:, :lanes], f[:, lanes:]
            products.append(
                jnp.concatenate([f_re * s_re - f_im * s_im, f_re * s_im + f_im * s_re], axis=1).astype(BF16)
            )
        back = dot(jnp.concatenate(products, axis=0), second_back)
        unturned = []
        for h in range(TOGETHER):
            re = back[h * blocks : (h + 1) * blocks, :lanes]
            im = back[h * blocks : (h + 1) * blocks, lanes:]
            unturned.append(jnp.concatenate([re * cos - im * sin, im * cos + re * sin], axis=0).astype(BF16))
        for j in range(0, TOGETHER, 2):
            y = dot(first_back, jnp.concatenate(unturned[j : j + 2], axis=1))
            for h in range(2):
                c = begin + j + h
                inner = y[:, h * lanes : (h + 1) * lanes] + columns[c : c + 1, 24:25] * signals[j + h]
                long_s[pl.ds(c, blocks, stride=pitch), :] = channel(gate, c, pitch).T * inner

    def round_step(b, carry):
        out_ref[pl.ds(pl.multiple_of(b * width, width), width), :] = long_s[pl.ds(b * pitch, width), :].astype(BF16)
        return carry

    lax.fori_loop(0, blocks, round_step, 0, unroll=8)


def conv_call(me, arrived, chunk0, chunk1, chunk2, columns, constants, tap_count):
    blocks, rows_in, positions = arrived.shape
    width, vocab = chunk0.shape
    rows = 3 * width
    pitch = width + 1
    vmem = pl.BlockSpec(memory_space=pltpu.VMEM)
    spectrum, codes = pl.pallas_call(
        functools.partial(filter_kernel, pitch=pitch),
        in_specs=[vmem] * 2,
        out_specs=[vmem] * 2,
        out_shape=[
            jax.ShapeDtypeStruct((width * blocks, 2 * positions), BF16),
            jax.ShapeDtypeStruct((positions, blocks), F32),
        ],
        scratch_shapes=[pltpu.VMEM((blocks * pitch, positions), F32)],
        compiler_params=pltpu.CompilerParams(vmem_limit_bytes=16 * 1024 * 1024),
        name="filter_spectrum",
    )(arrived, constants)
    return pl.pallas_call(
        functools.partial(conv_kernel, tap_count=tap_count, pitch=pitch),
        in_specs=[pl.BlockSpec(memory_space=pltpu.SMEM)] + [vmem] * 7,
        out_specs=vmem,
        out_shape=jax.ShapeDtypeStruct((blocks * width, positions), BF16),
        scratch_shapes=[
            pltpu.VMEM((positions * pitch, blocks), F32),
            pltpu.VMEM((positions * pitch, blocks), F32),
            pltpu.VMEM(((positions + 8) * rows, blocks), F32),
            pltpu.VMEM((blocks * pitch, positions), F32),
            pltpu.VMEM((3, width, vocab), BF16),
        ],
        compiler_params=pltpu.CompilerParams(vmem_limit_bytes=32 * 1024 * 1024),
        name="convolution",
    )(me, spectrum, codes, chunk0, chunk1, chunk2, columns, constants)


def local(token_ids, embedding, norm_gain, w_in, short_taps, long_filter, skip_gain):
    devices = lax.axis_size(AXES)
    me = lax.axis_index(AXES)
    positions, channels = long_filter.shape
    width = channels // devices
    vocab = embedding.shape[0]
    half = vocab // 2
    blocks = devices
    rows = 3 * width
    constants = transform_tables(blocks, positions)

    vmem = pl.BlockSpec(memory_space=pltpu.VMEM)
    hbm = pl.BlockSpec(memory_space=pltpu.HBM)
    sent = pl.pallas_call(
        functools.partial(pack_kernel, half=half),
        in_specs=[hbm, hbm],
        out_specs=vmem,
        out_shape=jax.ShapeDtypeStruct((devices, width + 1, positions), BF16),
        scratch_shapes=[
            pltpu.VMEM((positions, channels), F32),
            pltpu.VMEM((1, positions), jnp.int32),
            pltpu.SemaphoreType.DMA((5,)),
        ],
        compiler_params=pltpu.CompilerParams(vmem_limit_bytes=PACK_VMEM * 1024 * 1024),
        name="pack",
    )(long_filter, token_ids[None])
    arrived = lax.all_to_all(sent, AXES, split_axis=0, concat_axis=0, tiled=True)

    block = (3 * me % devices)[None].astype(jnp.int32)
    *own, columns = pl.pallas_call(
        table_kernel,
        in_specs=[pl.BlockSpec(memory_space=pltpu.SMEM), vmem, vmem, vmem, hbm, hbm],
        out_specs=[vmem] * 4,
        out_shape=[jax.ShapeDtypeStruct((width, vocab), BF16)] * 3 + [jax.ShapeDtypeStruct((width, LANES), F32)],
        scratch_shapes=[
            pltpu.VMEM((LANES, embedding.shape[1]), BF16),
            pltpu.VMEM((8, embedding.shape[1]), F32),
            pltpu.VMEM((LANES, LANES), F32),
            pltpu.SemaphoreType.DMA((4,)),
        ],
        compiler_params=pltpu.CompilerParams(vmem_limit_bytes=TABLE_VMEM * 1024 * 1024),
        name="table",
    )(block, embedding, norm_gain[None], w_in.T, short_taps, skip_gain.reshape(channels // LANES, LANES))
    inverse = pow(3, -1, devices)
    chunks = [own[0]] + [
        lax.ppermute(own[j], AXES, [(d, (d + j * inverse) % devices) for d in range(devices)]) for j in (1, 2)
    ]

    out = conv_call(block, arrived, *chunks, columns, constants, short_taps.shape[0])
    received = lax.all_to_all(
        out.reshape(devices, width, positions), AXES, split_axis=0, concat_axis=0, tiled=True
    )
    return pl.pallas_call(
        unpack_kernel,
        in_specs=[vmem],
        out_specs=vmem,
        out_shape=jax.ShapeDtypeStruct((positions, channels), BF16),
        compiler_params=pltpu.CompilerParams(vmem_limit_bytes=16 * 1024 * 1024),
        name="unpack",
    )(received)


def solution(mesh):
    in_specs = (
        P(AXES),
        P(),
        P(),
        P(None, AXES),
        P(),
        P(AXES, None),
        P(),
    )
    out_specs = P(AXES, None)
    return jax.shard_map(local, mesh=mesh, in_specs=in_specs, out_specs=out_specs, check_vma=False)
```

```python
import functools

import jax
import jax.numpy as jnp
import numpy as np
from jax import lax
from jax.experimental import pallas as pl
from jax.experimental.pallas import tpu as pltpu
from jax.sharding import PartitionSpec as P

AXES = ("row", "col")
EPSILON = 1e-05
LANES = 128
AT_ONCE = 32
PACK_VMEM = 62
TABLE_VMEM = 20
TOGETHER = 8
F32 = jnp.float32
BF16 = jnp.bfloat16


def transform_tables(blocks, lanes):
    n = blocks * lanes
    k = np.arange(blocks)
    angle_one = 2.0 * np.pi * np.outer(4 * k + 1, np.arange(blocks)) / (4 * blocks)
    angle_twist = 2.0 * np.pi * np.outer(4 * k + 1, np.arange(lanes)) / (4 * n)
    angle_two = 2.0 * np.pi * np.outer(np.arange(lanes), np.arange(lanes)) / lanes
    one = np.concatenate([np.cos(angle_one), -np.sin(angle_one)], axis=1)
    two = np.concatenate([np.cos(angle_two), np.sin(angle_two)], axis=1)
    back = np.concatenate([np.cos(angle_one).T, -np.sin(angle_one).T], axis=1) / n
    rounded = np.concatenate([one, two, back], axis=0).astype(np.float32).astype(jnp.bfloat16).astype(np.float32)
    twist = np.concatenate([np.cos(angle_twist), np.sin(angle_twist)], axis=1).astype(np.float32)
    return np.concatenate([twist, rounded], axis=0)


def dot(a, b):
    return jnp.dot(a, b, preferred_element_type=F32)


def table_kernel(
    me_ref, embedding_ref, gain_ref, w_ref, taps_hbm, skip_hbm, out0_ref, out1_ref, out2_ref, columns_ref,
    normed, gain_wide, small, small_arrived,
):
    vocab, depth = embedding_ref.shape
    width = out0_ref.shape[0]
    tap_count = taps_hbm.shape[0]
    channels = taps_hbm.shape[1] // 3
    share = LANES // width
    me = me_ref[0]
    few = [pltpu.make_async_copy(skip_hbm.at[pl.ds(me // share, 1), :], small.at[pl.ds(24, 1), :], small_arrived.at[3])]
    for g in range(3):
        at = pl.ds(pl.multiple_of(g * channels + me // share * LANES, LANES), LANES)
        few.append(
            pltpu.make_async_copy(taps_hbm.at[:, at], small.at[pl.ds(8 * g, tap_count), :], small_arrived.at[g])
        )
    for copy in few:
        copy.start()
    gain_wide[...] = jnp.broadcast_to(gain_ref[...].astype(F32), gain_wide.shape)
    for copy in few:
        copy.wait()
    small[...] = small[...].T
    columns_ref[...] = small[pl.ds(pl.multiple_of(me % share * width, 8), width), :]

    @pl.loop(0, vocab // LANES)
    def _(part):
        begin = pl.multiple_of(part * LANES, LANES)

        def norm_step(i, carry):
            x = embedding_ref[pl.ds(pl.multiple_of(begin + i * 16, 16), 16), :].astype(F32)
            inverse_rms = lax.rsqrt(jnp.mean(x * x, axis=1, keepdims=True) + EPSILON)
            gain = jnp.concatenate([gain_wide[...]] * 2, axis=0)
            normed[pl.ds(pl.multiple_of(i * 16, 16), 16), :] = (x * inverse_rms * gain).astype(BF16)
            return carry

        lax.fori_loop(0, LANES // 16, norm_step, 0, unroll=8)
        product = lax.dot_general(
            w_ref[...], normed[...], (((1,), (1,)), ((), ())), preferred_element_type=F32
        ).astype(BF16)
        for j, out_ref in enumerate((out0_ref, out1_ref, out2_ref)):
            out_ref[:, pl.ds(begin, LANES)] = product[j * width : (j + 1) * width]


def pack_kernel(filter_hbm, ids_hbm, out_ref, filter_ref, ids_ref, arrived, *, half):
    count, rows, positions = out_ref.shape
    width = rows - 1
    group = LANES // width
    part = filter_hbm.shape[1] // 4
    copies = [pltpu.make_async_copy(ids_hbm, ids_ref, arrived.at[4])]
    for k in range(4):
        at = pl.ds(k * part, part)
        copies.append(pltpu.make_async_copy(filter_hbm.at[:, at], filter_ref.at[:, at], arrived.at[k]))
    for copy in copies:
        copy.start()
    copies[0].wait()
    ids = ids_ref[...]
    code = jnp.where(ids < half, ids + 1, half - 1 - ids).astype(F32).astype(BF16)
    inverse = pow(3, -1, count)
    for q in range(0, count, group):
        if q * width % part == 0:
            copies[1 + q * width // part].wait()
        turned = filter_ref[:, q * width : (q + group) * width].T.astype(BF16)
        for e in range(group):
            out_ref[(q + e) * inverse % count] = jnp.concatenate(
                [turned[e * width : (e + 1) * width], code], axis=0
            )


def unpack_kernel(received_ref, out_hbm, out_ref, sent):
    count, width, positions = received_ref.shape
    inverse = pow(3, -1, count)
    group = LANES // width
    part = out_ref.shape[1] // 4
    copies = []
    for q in range(0, count, group):
        rows = [received_ref[(q + e) * inverse % count].astype(F32) for e in range(group)]
        out_ref[:, q * width : (q + group) * width] = jnp.concatenate(rows, axis=0).T.astype(BF16)
        end = (q + group) * width
        if end % part == 0:
            at = pl.ds(end - part, part)
            copies.append(pltpu.make_async_copy(out_ref.at[:, at], out_hbm.at[:, at], sent.at[len(copies)]))
            copies[-1].start()
    for copy in copies:
        copy.wait()


def matrices(constants_ref):
    lanes = LANES
    blocks = (constants_ref.shape[0] - lanes) // 3
    cos = constants_ref[:blocks, :lanes]
    sin = constants_ref[:blocks, lanes:]
    one = constants_ref[blocks : 2 * blocks, :].astype(BF16)
    first = jnp.concatenate([one[:, :blocks], one[:, blocks:]], axis=0)
    two = constants_ref[2 * blocks : 2 * blocks + lanes, :]
    real, imaginary = two[:, :lanes].astype(BF16), two[:, lanes:].astype(BF16)
    minus = (-two[:, lanes:]).astype(BF16)
    second = jnp.concatenate(
        [jnp.concatenate([real, minus], axis=1), jnp.concatenate([imaginary, real], axis=1)], axis=0
    )
    second_back = jnp.concatenate(
        [jnp.concatenate([real, imaginary], axis=1), jnp.concatenate([minus, real], axis=1)], axis=0
    )
    first_back = constants_ref[2 * blocks + lanes :, :].astype(BF16)
    return cos, sin, first, second, second_back, first_back


def channel(ref, c, pitch):
    return ref[pl.ds(c, ref.shape[0] // pitch, stride=pitch), :]


def forward(series, cos, sin, first, second):
    blocks, lanes = cos.shape
    turned = []
    for j in range(0, len(series), 2):
        a = dot(first, jnp.concatenate(series[j : j + 2], axis=1).astype(BF16))
        for h in range(2):
            re = a[:blocks, h * lanes : (h + 1) * lanes]
            im = a[blocks:, h * lanes : (h + 1) * lanes]
            turned.append(jnp.concatenate([re * cos + im * sin, im * cos - re * sin], axis=1).astype(BF16))
    return dot(jnp.concatenate(turned, axis=0), second)


def filter_kernel(arrived_ref, constants_ref, spectrum_ref, codes_ref, filter_s, *, pitch):
    blocks, rows_in, lanes = arrived_ref.shape
    width = rows_in - 1

    def cast_step(b, carry):
        got = arrived_ref[b].astype(F32)
        filter_s[pl.ds(b * pitch, width), :] = got[:width]
        codes_ref[pl.ds(b, 1), :] = got[width:]
        return carry

    lax.fori_loop(0, blocks, cast_step, 0, unroll=8)
    codes_ref[...] = codes_ref[...].T
    cos, sin, first, second, _, _ = matrices(constants_ref)
    for c in range(0, width, TOGETHER):
        z = forward([channel(filter_s, c + h, pitch) for h in range(TOGETHER)], cos, sin, first, second)
        spectrum_ref[c * blocks : (c + TOGETHER) * blocks, :] = z.astype(BF16)


def conv_kernel(
    me_ref, spectrum_ref, codes_s, chunk0_ref, chunk1_ref, chunk2_ref, columns_ref, constants_ref, out_ref,
    gate, signal, mixed, long_s, chunks, *, tap_count, pitch,
):
    blocks, lanes = codes_s.shape[::-1]
    width = chunk0_ref.shape[0]
    rows = 3 * width
    vocab = chunk0_ref.shape[1]
    half = vocab // 2
    me = me_ref[0]
    columns = columns_ref[...]

    chunks[0] = chunk0_ref[...]
    chunks[1] = chunk1_ref[...]
    chunks[2] = chunk2_ref[...]
    parts = [chunks[(me + g * blocks) % 3] for g in range(3)]
    folded = jnp.concatenate([x[:, :half] for x in parts] + [x[:, half:] for x in parts], axis=0)

    entry = (lax.broadcasted_iota(jnp.int32, (16, blocks), 0).astype(F32) + 1.0).astype(BF16)

    def look_up(positions):
        found = []
        hots = []
        for p in positions:
            code = codes_s[p : p + 1, :]
            found.append(code)
            size = jnp.broadcast_to(jnp.abs(code), (16, blocks)).astype(BF16)
            equal = [jnp.where(entry == size - BF16(r), BF16(1), BF16(0)).astype(BF16) for r in range(0, half, 16)]
            hots.append(jnp.concatenate(equal, axis=0))
        both = dot(folded, jnp.concatenate(hots, axis=1))
        for h, p in enumerate(positions):
            here = both[:, h * blocks : (h + 1) * blocks]
            mixed[(p + 8) * rows : (p + 9) * rows, :] = jnp.where(found[h] < 0.0, here[rows:], here[:rows])

    def short_filter(positions):
        for c in range(0, width, 8):
            taps = [
                [jnp.broadcast_to(columns[c : c + 8, 8 * g + i : 8 * g + i + 1], (8, blocks)) for i in range(tap_count)]
                for g in range(3)
            ]

            def at(p, g):
                begin = (p + 8) * rows + g * width + c
                return mixed[begin : begin + 8, :]

            window = [[at(positions[0] - i, g) for i in range(1, tap_count)] for g in range(3)]
            for p in positions:
                total = []
                for g in range(3):
                    here = at(p, g)
                    value = taps[g][0] * here
                    for i in range(1, tap_count):
                        value = value + taps[g][i] * window[g][i - 1]
                    total.append(value)
                    window[g] = [here] + window[g][:-1]
                gate[p * pitch + c : p * pitch + c + 8, :] = total[0]
                signal[p * pitch + c : p * pitch + c + 8, :] = total[1] * total[2]

    steps = [range(p, p + AT_ONCE) for p in range(0, lanes, AT_ONCE)]
    look_up(steps[-1])
    block = lax.broadcasted_iota(jnp.int32, (rows, blocks), 1)
    for i in range(1, tap_count):
        last = mixed[(lanes + 8 - i) * rows : (lanes + 9 - i) * rows, :]
        mixed[(8 - i) * rows : (9 - i) * rows, :] = jnp.where(block == 0, 0.0, pltpu.roll(last, 1, 1))
    for k, step in enumerate(steps):
        if k == 0:
            look_up(step)
        if k + 1 < len(steps) - 1:
            look_up(steps[k + 1])
        short_filter(step)

    cos, sin, first, second, second_back, first_back = matrices(constants_ref)

    for begin in range(0, width, TOGETHER):
        signals = [channel(signal, begin + h, pitch).T for h in range(TOGETHER)]
        z = forward(signals, cos, sin, first, second)
        products = []
        for h in range(TOGETHER):
            s = z[h * blocks : (h + 1) * blocks]
            f = spectrum_ref[(begin + h) * blocks : (begin + h + 1) * blocks, :].astype(F32)
            s_re, s_im, f_re, f_im = s[:, :lanes], s[:, lanes:], f[:, :lanes], f[:, lanes:]
            products.append(
                jnp.concatenate([f_re * s_re - f_im * s_im, f_re * s_im + f_im * s_re], axis=1).astype(BF16)
            )
        back = dot(jnp.concatenate(products, axis=0), second_back)
        unturned = []
        for h in range(TOGETHER):
            re = back[h * blocks : (h + 1) * blocks, :lanes]
            im = back[h * blocks : (h + 1) * blocks, lanes:]
            unturned.append(jnp.concatenate([re * cos - im * sin, im * cos + re * sin], axis=0).astype(BF16))
        for j in range(0, TOGETHER, 2):
            y = dot(first_back, jnp.concatenate(unturned[j : j + 2], axis=1))
            for h in range(2):
                c = begin + j + h
                inner = y[:, h * lanes : (h + 1) * lanes] + columns[c : c + 1, 24:25] * signals[j + h]
                long_s[pl.ds(c, blocks, stride=pitch), :] = channel(gate, c, pitch).T * inner

    def round_step(b, carry):
        out_ref[pl.ds(pl.multiple_of(b * width, width), width), :] = long_s[pl.ds(b * pitch, width), :].astype(BF16)
        return carry

    lax.fori_loop(0, blocks, round_step, 0, unroll=8)


def conv_call(me, arrived, chunk0, chunk1, chunk2, columns, constants, tap_count):
    blocks, rows_in, positions = arrived.shape
    width, vocab = chunk0.shape
    rows = 3 * width
    pitch = width + 1
    vmem = pl.BlockSpec(memory_space=pltpu.VMEM)
    spectrum, codes = pl.pallas_call(
        functools.partial(filter_kernel, pitch=pitch),
        in_specs=[vmem] * 2,
        out_specs=[vmem] * 2,
        out_shape=[
            jax.ShapeDtypeStruct((width * blocks, 2 * positions), BF16),
            jax.ShapeDtypeStruct((positions, blocks), F32),
        ],
        scratch_shapes=[pltpu.VMEM((blocks * pitch, positions), F32)],
        compiler_params=pltpu.CompilerParams(vmem_limit_bytes=16 * 1024 * 1024),
        name="filter_spectrum",
    )(arrived, constants)
    return pl.pallas_call(
        functools.partial(conv_kernel, tap_count=tap_count, pitch=pitch),
        in_specs=[pl.BlockSpec(memory_space=pltpu.SMEM)] + [vmem] * 7,
        out_specs=vmem,
        out_shape=jax.ShapeDtypeStruct((blocks * width, positions), BF16),
        scratch_shapes=[
            pltpu.VMEM((positions * pitch, blocks), F32),
            pltpu.VMEM((positions * pitch, blocks), F32),
            pltpu.VMEM(((positions + 8) * rows, blocks), F32),
            pltpu.VMEM((blocks * pitch, positions), F32),
            pltpu.VMEM((3, width, vocab), BF16),
        ],
        compiler_params=pltpu.CompilerParams(vmem_limit_bytes=32 * 1024 * 1024),
        name="convolution",
    )(me, spectrum, codes, chunk0, chunk1, chunk2, columns, constants)


def local(token_ids, embedding, norm_gain, w_in, short_taps, long_filter, skip_gain):
    devices = lax.axis_size(AXES)
    me = lax.axis_index(AXES)
    positions, channels = long_filter.shape
    width = channels // devices
    vocab = embedding.shape[0]
    half = vocab // 2
    blocks = devices
    rows = 3 * width
    constants = transform_tables(blocks, positions)

    vmem = pl.BlockSpec(memory_space=pltpu.VMEM)
    hbm = pl.BlockSpec(memory_space=pltpu.HBM)
    sent = pl.pallas_call(
        functools.partial(pack_kernel, half=half),
        in_specs=[hbm, hbm],
        out_specs=vmem,
        out_shape=jax.ShapeDtypeStruct((devices, width + 1, positions), BF16),
        scratch_shapes=[
            pltpu.VMEM((positions, channels), F32),
            pltpu.VMEM((1, positions), jnp.int32),
            pltpu.SemaphoreType.DMA((5,)),
        ],
        compiler_params=pltpu.CompilerParams(vmem_limit_bytes=PACK_VMEM * 1024 * 1024),
        name="pack",
    )(long_filter, token_ids[None])
    arrived = lax.all_to_all(sent, AXES, split_axis=0, concat_axis=0, tiled=True)

    block = (3 * me % devices)[None].astype(jnp.int32)
    *own, columns = pl.pallas_call(
        table_kernel,
        in_specs=[pl.BlockSpec(memory_space=pltpu.SMEM), vmem, vmem, vmem, hbm, hbm],
        out_specs=[vmem] * 4,
        out_shape=[jax.ShapeDtypeStruct((width, vocab), BF16)] * 3 + [jax.ShapeDtypeStruct((width, LANES), F32)],
        scratch_shapes=[
            pltpu.VMEM((LANES, embedding.shape[1]), BF16),
            pltpu.VMEM((8, embedding.shape[1]), F32),
            pltpu.VMEM((LANES, LANES), F32),
            pltpu.SemaphoreType.DMA((4,)),
        ],
        compiler_params=pltpu.CompilerParams(vmem_limit_bytes=TABLE_VMEM * 1024 * 1024),
        name="table",
    )(block, embedding, norm_gain[None], w_in.T, short_taps, skip_gain.reshape(channels // LANES, LANES))
    inverse = pow(3, -1, devices)
    chunks = [own[0]] + [
        lax.ppermute(own[j], AXES, [(d, (d + j * inverse) % devices) for d in range(devices)]) for j in (1, 2)
    ]

    out = conv_call(block, arrived, *chunks, columns, constants, short_taps.shape[0])
    received = lax.all_to_all(
        out.reshape(devices, width, positions), AXES, split_axis=0, concat_axis=0, tiled=True
    )
    return pl.pallas_call(
        unpack_kernel,
        in_specs=[vmem],
        out_specs=hbm,
        out_shape=jax.ShapeDtypeStruct((positions, channels), BF16),
        scratch_shapes=[pltpu.VMEM((positions, channels), BF16), pltpu.SemaphoreType.DMA((4,))],
        compiler_params=pltpu.CompilerParams(vmem_limit_bytes=16 * 1024 * 1024),
        name="unpack",
    )(received)


def solution(mesh):
    in_specs = (
        P(AXES),
        P(),
        P(),
        P(None, AXES),
        P(),
        P(AXES, None),
        P(),
    )
    out_specs = P(AXES, None)
    return jax.shard_map(local, mesh=mesh, in_specs=in_specs, out_specs=out_specs, check_vma=False)
```

```python
import functools

import jax
import jax.numpy as jnp
import numpy as np
from jax import lax
from jax.experimental import pallas as pl
from jax.experimental.pallas import tpu as pltpu
from jax.sharding import PartitionSpec as P

AXES = ("row", "col")
EPSILON = 1e-05
LANES = 128
AT_ONCE = 32
PACK_VMEM = 62
TABLE_VMEM = 20
TOGETHER = 16
F32 = jnp.float32
BF16 = jnp.bfloat16


def transform_tables(blocks, lanes):
    n = blocks * lanes
    k = np.arange(blocks)
    angle_one = 2.0 * np.pi * np.outer(4 * k + 1, np.arange(blocks)) / (4 * blocks)
    angle_twist = 2.0 * np.pi * np.outer(4 * k + 1, np.arange(lanes)) / (4 * n)
    angle_two = 2.0 * np.pi * np.outer(np.arange(lanes), np.arange(lanes)) / lanes
    one = np.concatenate([np.cos(angle_one), -np.sin(angle_one)], axis=1)
    two = np.concatenate([np.cos(angle_two), np.sin(angle_two)], axis=1)
    back = np.concatenate([np.cos(angle_one).T, -np.sin(angle_one).T], axis=1) / n
    rounded = np.concatenate([one, two, back], axis=0).astype(np.float32).astype(jnp.bfloat16).astype(np.float32)
    twist = np.concatenate([np.cos(angle_twist), np.sin(angle_twist)], axis=1).astype(np.float32)
    return np.concatenate([twist, rounded], axis=0)


def dot(a, b):
    return jnp.dot(a, b, preferred_element_type=F32)


def table_kernel(
    me_ref, embedding_ref, gain_ref, w_ref, taps_hbm, skip_hbm, out0_ref, out1_ref, out2_ref, columns_ref,
    normed, gain_wide, small, small_arrived,
):
    vocab, depth = embedding_ref.shape
    width = out0_ref.shape[0]
    tap_count = taps_hbm.shape[0]
    channels = taps_hbm.shape[1] // 3
    share = LANES // width
    me = me_ref[0]
    few = [pltpu.make_async_copy(skip_hbm.at[pl.ds(me // share, 1), :], small.at[pl.ds(24, 1), :], small_arrived.at[3])]
    for g in range(3):
        at = pl.ds(pl.multiple_of(g * channels + me // share * LANES, LANES), LANES)
        few.append(
            pltpu.make_async_copy(taps_hbm.at[:, at], small.at[pl.ds(8 * g, tap_count), :], small_arrived.at[g])
        )
    for copy in few:
        copy.start()
    gain_wide[...] = jnp.broadcast_to(gain_ref[...].astype(F32), gain_wide.shape)
    for copy in few:
        copy.wait()
    small[...] = small[...].T
    columns_ref[...] = small[pl.ds(pl.multiple_of(me % share * width, 8), width), :]

    @pl.loop(0, vocab // LANES)
    def _(part):
        begin = pl.multiple_of(part * LANES, LANES)

        def norm_step(i, carry):
            x = embedding_ref[pl.ds(pl.multiple_of(begin + i * 16, 16), 16), :].astype(F32)
            inverse_rms = lax.rsqrt(jnp.mean(x * x, axis=1, keepdims=True) + EPSILON)
            gain = jnp.concatenate([gain_wide[...]] * 2, axis=0)
            normed[pl.ds(pl.multiple_of(i * 16, 16), 16), :] = (x * inverse_rms * gain).astype(BF16)
            return carry

        lax.fori_loop(0, LANES // 16, norm_step, 0, unroll=8)
        product = lax.dot_general(
            w_ref[...], normed[...], (((1,), (1,)), ((), ())), preferred_element_type=F32
        ).astype(BF16)
        for j, out_ref in enumerate((out0_ref, out1_ref, out2_ref)):
            out_ref[:, pl.ds(begin, LANES)] = product[j * width : (j + 1) * width]


def pack_kernel(filter_hbm, ids_hbm, out_ref, filter_ref, ids_ref, arrived, *, half):
    count, rows, positions = out_ref.shape
    width = rows - 1
    group = LANES // width
    part = filter_hbm.shape[1] // 4
    copies = [pltpu.make_async_copy(ids_hbm, ids_ref, arrived.at[4])]
    for k in range(4):
        at = pl.ds(k * part, part)
        copies.append(pltpu.make_async_copy(filter_hbm.at[:, at], filter_ref.at[:, at], arrived.at[k]))
    for copy in copies:
        copy.start()
    copies[0].wait()
    ids = ids_ref[...]
    code = jnp.where(ids < half, ids + 1, half - 1 - ids).astype(F32).astype(BF16)
    inverse = pow(3, -1, count)
    for q in range(0, count, group):
        if q * width % part == 0:
            copies[1 + q * width // part].wait()
        turned = filter_ref[:, q * width : (q + group) * width].T.astype(BF16)
        for e in range(group):
            out_ref[(q + e - 1) * inverse % count] = jnp.concatenate(
                [turned[e * width : (e + 1) * width], code], axis=0
            )


def unpack_kernel(received_ref, out_hbm, out_ref, sent):
    count, width, positions = received_ref.shape
    inverse = pow(3, -1, count)
    group = LANES // width
    part = out_ref.shape[1] // 4
    copies = []
    for q in range(0, count, group):
        rows = [received_ref[(q + e - 1) * inverse % count].astype(F32) for e in range(group)]
        out_ref[:, q * width : (q + group) * width] = jnp.concatenate(rows, axis=0).T.astype(BF16)
        end = (q + group) * width
        if end % part == 0:
            at = pl.ds(end - part, part)
            copies.append(pltpu.make_async_copy(out_ref.at[:, at], out_hbm.at[:, at], sent.at[len(copies)]))
            copies[-1].start()
    for copy in copies:
        copy.wait()


def matrices(constants_ref):
    lanes = LANES
    blocks = (constants_ref.shape[0] - lanes) // 3
    cos = constants_ref[:blocks, :lanes]
    sin = constants_ref[:blocks, lanes:]
    one = constants_ref[blocks : 2 * blocks, :].astype(BF16)
    first = jnp.concatenate([one[:, :blocks], one[:, blocks:]], axis=0)
    two = constants_ref[2 * blocks : 2 * blocks + lanes, :]
    real, imaginary = two[:, :lanes].astype(BF16), two[:, lanes:].astype(BF16)
    minus = (-two[:, lanes:]).astype(BF16)
    second = jnp.concatenate(
        [jnp.concatenate([real, minus], axis=1), jnp.concatenate([imaginary, real], axis=1)], axis=0
    )
    second_back = jnp.concatenate(
        [jnp.concatenate([real, imaginary], axis=1), jnp.concatenate([minus, real], axis=1)], axis=0
    )
    first_back = constants_ref[2 * blocks + lanes :, :].astype(BF16)
    return cos, sin, first, second, second_back, first_back


def channel(ref, c, pitch):
    return ref[pl.ds(c, ref.shape[0] // pitch, stride=pitch), :]


def forward(series, cos, sin, first, second):
    blocks, lanes = cos.shape
    turned = []
    for j in range(0, len(series), 2):
        a = dot(first, jnp.concatenate(series[j : j + 2], axis=1).astype(BF16))
        for h in range(2):
            re = a[:blocks, h * lanes : (h + 1) * lanes]
            im = a[blocks:, h * lanes : (h + 1) * lanes]
            turned.append(jnp.concatenate([re * cos + im * sin, im * cos - re * sin], axis=1).astype(BF16))
    return dot(jnp.concatenate(turned, axis=0), second)


def filter_kernel(arrived_ref, constants_ref, spectrum_ref, codes_ref, filter_s, *, pitch):
    blocks, rows_in, lanes = arrived_ref.shape
    width = rows_in - 1

    def cast_step(b, carry):
        got = arrived_ref[b].astype(F32)
        filter_s[pl.ds(b * pitch, width), :] = got[:width]
        codes_ref[pl.ds(b, 1), :] = got[width:]
        return carry

    lax.fori_loop(0, blocks, cast_step, 0, unroll=8)
    codes_ref[...] = codes_ref[...].T
    cos, sin, first, second, _, _ = matrices(constants_ref)
    for c in range(0, width, TOGETHER):
        z = forward([channel(filter_s, c + h, pitch) for h in range(TOGETHER)], cos, sin, first, second)
        spectrum_ref[c * blocks : (c + TOGETHER) * blocks, :] = z.astype(BF16)


def conv_kernel(
    me_ref, spectrum_ref, codes_s, chunk0_ref, chunk1_ref, chunk2_ref, columns_ref, constants_ref, out_ref,
    gate, signal, mixed, long_s, chunks, *, tap_count, pitch,
):
    blocks, lanes = codes_s.shape[::-1]
    width = chunk0_ref.shape[0]
    rows = 3 * width
    vocab = chunk0_ref.shape[1]
    half = vocab // 2
    me = me_ref[0]
    columns = columns_ref[...]

    chunks[0] = chunk0_ref[...]
    chunks[1] = chunk1_ref[...]
    chunks[2] = chunk2_ref[...]
    parts = [chunks[(me + g * blocks) % 3] for g in range(3)]
    folded = jnp.concatenate([x[:, :half] for x in parts] + [x[:, half:] for x in parts], axis=0)

    entry = (lax.broadcasted_iota(jnp.int32, (16, blocks), 0).astype(F32) + 1.0).astype(BF16)

    def look_up(positions):
        found = []
        hots = []
        for p in positions:
            code = codes_s[p : p + 1, :]
            found.append(code)
            size = jnp.broadcast_to(jnp.abs(code), (16, blocks)).astype(BF16)
            equal = [jnp.where(entry == size - BF16(r), BF16(1), BF16(0)).astype(BF16) for r in range(0, half, 16)]
            hots.append(jnp.concatenate(equal, axis=0))
        both = dot(folded, jnp.concatenate(hots, axis=1))
        for h, p in enumerate(positions):
            here = both[:, h * blocks : (h + 1) * blocks]
            mixed[(p + 8) * rows : (p + 9) * rows, :] = jnp.where(found[h] < 0.0, here[rows:], here[:rows])

    def short_filter(positions):
        for c in range(0, width, 8):
            taps = [
                [jnp.broadcast_to(columns[c : c + 8, 8 * g + i : 8 * g + i + 1], (8, blocks)) for i in range(tap_count)]
                for g in range(3)
            ]

            def at(p, g):
                begin = (p + 8) * rows + g * width + c
                return mixed[begin : begin + 8, :]

            window = [[at(positions[0] - i, g) for i in range(1, tap_count)] for g in range(3)]
            for p in positions:
                total = []
                for g in range(3):
                    here = at(p, g)
                    value = taps[g][0] * here
                    for i in range(1, tap_count):
                        value = value + taps[g][i] * window[g][i - 1]
                    total.append(value)
                    window[g] = [here] + window[g][:-1]
                gate[p * pitch + c : p * pitch + c + 8, :] = total[0]
                signal[p * pitch + c : p * pitch + c + 8, :] = total[1] * total[2]

    steps = [range(p, p + AT_ONCE) for p in range(0, lanes, AT_ONCE)]
    look_up(steps[-1])
    block = lax.broadcasted_iota(jnp.int32, (rows, blocks), 1)
    for i in range(1, tap_count):
        last = mixed[(lanes + 8 - i) * rows : (lanes + 9 - i) * rows, :]
        mixed[(8 - i) * rows : (9 - i) * rows, :] = jnp.where(block == 0, 0.0, pltpu.roll(last, 1, 1))
    for k, step in enumerate(steps):
        if k == 0:
            look_up(step)
        if k + 1 < len(steps) - 1:
            look_up(steps[k + 1])
        short_filter(step)

    cos, sin, first, second, second_back, first_back = matrices(constants_ref)

    for begin in range(0, width, TOGETHER):
        signals = [channel(signal, begin + h, pitch).T for h in range(TOGETHER)]
        z = forward(signals, cos, sin, first, second)
        products = []
        for h in range(TOGETHER):
            s = z[h * blocks : (h + 1) * blocks]
            f = spectrum_ref[(begin + h) * blocks : (begin + h + 1) * blocks, :].astype(F32)
            s_re, s_im, f_re, f_im = s[:, :lanes], s[:, lanes:], f[:, :lanes], f[:, lanes:]
            products.append(
                jnp.concatenate([f_re * s_re - f_im * s_im, f_re * s_im + f_im * s_re], axis=1).astype(BF16)
            )
        back = dot(jnp.concatenate(products, axis=0), second_back)
        unturned = []
        for h in range(TOGETHER):
            re = back[h * blocks : (h + 1) * blocks, :lanes]
            im = back[h * blocks : (h + 1) * blocks, lanes:]
            unturned.append(jnp.concatenate([re * cos - im * sin, im * cos + re * sin], axis=0).astype(BF16))
        for j in range(0, TOGETHER, 2):
            y = dot(first_back, jnp.concatenate(unturned[j : j + 2], axis=1))
            for h in range(2):
                c = begin + j + h
                inner = y[:, h * lanes : (h + 1) * lanes] + columns[c : c + 1, 24:25] * signals[j + h]
                long_s[pl.ds(c, blocks, stride=pitch), :] = channel(gate, c, pitch).T * inner

    def round_step(b, carry):
        out_ref[pl.ds(pl.multiple_of(b * width, width), width), :] = long_s[pl.ds(b * pitch, width), :].astype(BF16)
        return carry

    lax.fori_loop(0, blocks, round_step, 0, unroll=8)


def conv_call(me, arrived, chunk0, chunk1, chunk2, columns, constants, tap_count):
    blocks, rows_in, positions = arrived.shape
    width, vocab = chunk0.shape
    rows = 3 * width
    pitch = width + 1
    vmem = pl.BlockSpec(memory_space=pltpu.VMEM)
    spectrum, codes = pl.pallas_call(
        functools.partial(filter_kernel, pitch=pitch),
        in_specs=[vmem] * 2,
        out_specs=[vmem] * 2,
        out_shape=[
            jax.ShapeDtypeStruct((width * blocks, 2 * positions), BF16),
            jax.ShapeDtypeStruct((positions, blocks), F32),
        ],
        scratch_shapes=[pltpu.VMEM((blocks * pitch, positions), F32)],
        compiler_params=pltpu.CompilerParams(vmem_limit_bytes=16 * 1024 * 1024),
        name="filter_spectrum",
    )(arrived, constants)
    return pl.pallas_call(
        functools.partial(conv_kernel, tap_count=tap_count, pitch=pitch),
        in_specs=[pl.BlockSpec(memory_space=pltpu.SMEM)] + [vmem] * 7,
        out_specs=vmem,
        out_shape=jax.ShapeDtypeStruct((blocks * width, positions), BF16),
        scratch_shapes=[
            pltpu.VMEM((positions * pitch, blocks), F32),
            pltpu.VMEM((positions * pitch, blocks), F32),
            pltpu.VMEM(((positions + 8) * rows, blocks), F32),
            pltpu.VMEM((blocks * pitch, positions), F32),
            pltpu.VMEM((3, width, vocab), BF16),
        ],
        compiler_params=pltpu.CompilerParams(vmem_limit_bytes=32 * 1024 * 1024),
        name="convolution",
    )(me, spectrum, codes, chunk0, chunk1, chunk2, columns, constants)


def local(token_ids, embedding, norm_gain, w_in, short_taps, long_filter, skip_gain):
    devices = lax.axis_size(AXES)
    me = lax.axis_index(AXES)
    positions, channels = long_filter.shape
    width = channels // devices
    vocab = embedding.shape[0]
    half = vocab // 2
    blocks = devices
    rows = 3 * width
    constants = transform_tables(blocks, positions)

    vmem = pl.BlockSpec(memory_space=pltpu.VMEM)
    hbm = pl.BlockSpec(memory_space=pltpu.HBM)
    sent = pl.pallas_call(
        functools.partial(pack_kernel, half=half),
        in_specs=[hbm, hbm],
        out_specs=vmem,
        out_shape=jax.ShapeDtypeStruct((devices, width + 1, positions), BF16),
        scratch_shapes=[
            pltpu.VMEM((positions, channels), F32),
            pltpu.VMEM((1, positions), jnp.int32),
            pltpu.SemaphoreType.DMA((5,)),
        ],
        compiler_params=pltpu.CompilerParams(vmem_limit_bytes=PACK_VMEM * 1024 * 1024),
        name="pack",
    )(long_filter, token_ids[None])
    arrived = lax.all_to_all(sent, AXES, split_axis=0, concat_axis=0, tiled=True)

    block = ((3 * me + 1) % devices)[None].astype(jnp.int32)
    *own, columns = pl.pallas_call(
        table_kernel,
        in_specs=[pl.BlockSpec(memory_space=pltpu.SMEM), vmem, vmem, vmem, hbm, hbm],
        out_specs=[vmem] * 4,
        out_shape=[jax.ShapeDtypeStruct((width, vocab), BF16)] * 3 + [jax.ShapeDtypeStruct((width, LANES), F32)],
        scratch_shapes=[
            pltpu.VMEM((LANES, embedding.shape[1]), BF16),
            pltpu.VMEM((8, embedding.shape[1]), F32),
            pltpu.VMEM((LANES, LANES), F32),
            pltpu.SemaphoreType.DMA((4,)),
        ],
        compiler_params=pltpu.CompilerParams(vmem_limit_bytes=TABLE_VMEM * 1024 * 1024),
        name="table",
    )(block, embedding, norm_gain[None], w_in.T, short_taps, skip_gain.reshape(channels // LANES, LANES))
    inverse = pow(3, -1, devices)
    moved = [
        lax.ppermute(own[1 + j], AXES, [(d, (d + j * inverse) % devices) for d in range(devices)]) for j in (-1, 1)
    ]
    chunks = [moved[0], own[1], moved[1]]

    out = conv_call(block, arrived, *chunks, columns, constants, short_taps.shape[0])
    received = lax.all_to_all(
        out.reshape(devices, width, positions), AXES, split_axis=0, concat_axis=0, tiled=True
    )
    return pl.pallas_call(
        unpack_kernel,
        in_specs=[vmem],
        out_specs=hbm,
        out_shape=jax.ShapeDtypeStruct((positions, channels), BF16),
        scratch_shapes=[pltpu.VMEM((positions, channels), BF16), pltpu.SemaphoreType.DMA((4,))],
        compiler_params=pltpu.CompilerParams(vmem_limit_bytes=16 * 1024 * 1024),
        name="unpack",
    )(received)


def solution(mesh):
    in_specs = (
        P(AXES),
        P(),
        P(),
        P(None, AXES),
        P(),
        P(AXES, None),
        P(),
    )
    out_specs = P(AXES, None)
    return jax.shard_map(local, mesh=mesh, in_specs=in_specs, out_specs=out_specs, check_vma=False)
```

```python
import functools

import jax
import jax.numpy as jnp
import numpy as np
from jax import lax
from jax.experimental import pallas as pl
from jax.experimental.pallas import tpu as pltpu
from jax.sharding import PartitionSpec as P

AXES = ("row", "col")
EPSILON = 1e-05
LANES = 128
AT_ONCE = 32
PACK_VMEM = 62
PIECES = 2
TABLE_VMEM = 20
TOGETHER = 16
F32 = jnp.float32
BF16 = jnp.bfloat16


def transform_tables(blocks, lanes):
    n = blocks * lanes
    k = np.arange(blocks)
    angle_one = 2.0 * np.pi * np.outer(4 * k + 1, np.arange(blocks)) / (4 * blocks)
    angle_twist = 2.0 * np.pi * np.outer(4 * k + 1, np.arange(lanes)) / (4 * n)
    angle_two = 2.0 * np.pi * np.outer(np.arange(lanes), np.arange(lanes)) / lanes
    one = np.concatenate([np.cos(angle_one), -np.sin(angle_one)], axis=1)
    two = np.concatenate([np.cos(angle_two), np.sin(angle_two)], axis=1)
    back = np.concatenate([np.cos(angle_one).T, -np.sin(angle_one).T], axis=1) / n
    rounded = np.concatenate([one, two, back], axis=0).astype(np.float32).astype(jnp.bfloat16).astype(np.float32)
    twist = np.concatenate([np.cos(angle_twist), np.sin(angle_twist)], axis=1).astype(np.float32)
    return np.concatenate([twist, rounded], axis=0)


def dot(a, b):
    return jnp.dot(a, b, preferred_element_type=F32)


def table_kernel(
    me_ref, embedding_ref, gain_ref, w_ref, taps_hbm, skip_hbm, out0_ref, out1_ref, out2_ref, columns_ref,
    normed, gain_wide, small, small_arrived,
):
    vocab, depth = embedding_ref.shape
    width = out0_ref.shape[0]
    tap_count = taps_hbm.shape[0]
    channels = taps_hbm.shape[1] // 3
    share = LANES // width
    me = me_ref[0]
    few = [pltpu.make_async_copy(skip_hbm.at[pl.ds(me // share, 1), :], small.at[pl.ds(24, 1), :], small_arrived.at[3])]
    for g in range(3):
        at = pl.ds(pl.multiple_of(g * channels + me // share * LANES, LANES), LANES)
        few.append(
            pltpu.make_async_copy(taps_hbm.at[:, at], small.at[pl.ds(8 * g, tap_count), :], small_arrived.at[g])
        )
    for copy in few:
        copy.start()
    gain_wide[...] = jnp.broadcast_to(gain_ref[...].astype(F32), gain_wide.shape)
    for copy in few:
        copy.wait()
    small[...] = small[...].T
    columns_ref[...] = small[pl.ds(pl.multiple_of(me % share * width, 8), width), :]

    @pl.loop(0, vocab // LANES)
    def _(part):
        begin = pl.multiple_of(part * LANES, LANES)

        def norm_step(i, carry):
            x = embedding_ref[pl.ds(pl.multiple_of(begin + i * 16, 16), 16), :].astype(F32)
            inverse_rms = lax.rsqrt(jnp.mean(x * x, axis=1, keepdims=True) + EPSILON)
            gain = jnp.concatenate([gain_wide[...]] * 2, axis=0)
            normed[pl.ds(pl.multiple_of(i * 16, 16), 16), :] = (x * inverse_rms * gain).astype(BF16)
            return carry

        lax.fori_loop(0, LANES // 16, norm_step, 0, unroll=8)
        product = lax.dot_general(
            w_ref[...], normed[...], (((1,), (1,)), ((), ())), preferred_element_type=F32
        ).astype(BF16)
        for j, out_ref in enumerate((out0_ref, out1_ref, out2_ref)):
            out_ref[:, pl.ds(begin, LANES)] = product[j * width : (j + 1) * width]


def pack_kernel(filter_hbm, ids_hbm, out_ref, filter_ref, ids_ref, arrived, *, half):
    count, rows, positions = out_ref.shape
    width = rows - 1
    group = LANES // width
    part = filter_hbm.shape[1] // PIECES
    copies = [pltpu.make_async_copy(ids_hbm, ids_ref, arrived.at[PIECES])]
    for k in range(PIECES):
        at = pl.ds(k * part, part)
        copies.append(pltpu.make_async_copy(filter_hbm.at[:, at], filter_ref.at[:, at], arrived.at[k]))
    for copy in copies:
        copy.start()
    copies[0].wait()
    ids = ids_ref[...]
    code = jnp.where(ids < half, ids + 1, half - 1 - ids).astype(F32).astype(BF16)
    inverse = pow(3, -1, count)
    for q in range(0, count, group):
        if q * width % part == 0:
            copies[1 + q * width // part].wait()
        turned = filter_ref[:, q * width : (q + group) * width].T.astype(BF16)
        for e in range(group):
            out_ref[(q + e - 1) * inverse % count] = jnp.concatenate(
                [turned[e * width : (e + 1) * width], code], axis=0
            )


def unpack_kernel(received_ref, out_hbm, out_ref, sent):
    count, width, positions = received_ref.shape
    inverse = pow(3, -1, count)
    group = LANES // width
    part = out_ref.shape[1] // 4
    copies = []
    for q in range(0, count, group):
        rows = [received_ref[(q + e - 1) * inverse % count].astype(F32) for e in range(group)]
        out_ref[:, q * width : (q + group) * width] = jnp.concatenate(rows, axis=0).T.astype(BF16)
        end = (q + group) * width
        if end % part == 0:
            at = pl.ds(end - part, part)
            copies.append(pltpu.make_async_copy(out_ref.at[:, at], out_hbm.at[:, at], sent.at[len(copies)]))
            copies[-1].start()
    for copy in copies:
        copy.wait()


def matrices(constants_ref):
    lanes = LANES
    blocks = (constants_ref.shape[0] - lanes) // 3
    cos = constants_ref[:blocks, :lanes]
    sin = constants_ref[:blocks, lanes:]
    one = constants_ref[blocks : 2 * blocks, :].astype(BF16)
    first = jnp.concatenate([one[:, :blocks], one[:, blocks:]], axis=0)
    two = constants_ref[2 * blocks : 2 * blocks + lanes, :]
    real, imaginary = two[:, :lanes].astype(BF16), two[:, lanes:].astype(BF16)
    minus = (-two[:, lanes:]).astype(BF16)
    second = jnp.concatenate(
        [jnp.concatenate([real, minus], axis=1), jnp.concatenate([imaginary, real], axis=1)], axis=0
    )
    second_back = jnp.concatenate(
        [jnp.concatenate([real, imaginary], axis=1), jnp.concatenate([minus, real], axis=1)], axis=0
    )
    first_back = constants_ref[2 * blocks + lanes :, :].astype(BF16)
    return cos, sin, first, second, second_back, first_back


def channel(ref, c, pitch):
    return ref[pl.ds(c, ref.shape[0] // pitch, stride=pitch), :]


def forward(series, cos, sin, first, second):
    blocks, lanes = cos.shape
    turned = []
    for j in range(0, len(series), 2):
        a = dot(first, jnp.concatenate(series[j : j + 2], axis=1).astype(BF16))
        for h in range(2):
            re = a[:blocks, h * lanes : (h + 1) * lanes]
            im = a[blocks:, h * lanes : (h + 1) * lanes]
            turned.append(jnp.concatenate([re * cos + im * sin, im * cos - re * sin], axis=1).astype(BF16))
    return dot(jnp.concatenate(turned, axis=0), second)


def filter_kernel(arrived_ref, constants_ref, spectrum_ref, codes_ref, filter_s, *, pitch):
    blocks, rows_in, lanes = arrived_ref.shape
    width = rows_in - 1

    def cast_step(b, carry):
        got = arrived_ref[b].astype(F32)
        filter_s[pl.ds(b * pitch, width), :] = got[:width]
        codes_ref[pl.ds(b, 1), :] = got[width:]
        return carry

    lax.fori_loop(0, blocks, cast_step, 0, unroll=8)
    codes_ref[...] = codes_ref[...].T
    cos, sin, first, second, _, _ = matrices(constants_ref)
    for c in range(0, width, TOGETHER):
        z = forward([channel(filter_s, c + h, pitch) for h in range(TOGETHER)], cos, sin, first, second)
        spectrum_ref[c * blocks : (c + TOGETHER) * blocks, :] = z.astype(BF16)


def conv_kernel(
    me_ref, spectrum_ref, codes_s, chunk0_ref, chunk1_ref, chunk2_ref, columns_ref, constants_ref, out_ref,
    gate, signal, mixed, long_s, chunks, *, tap_count, pitch,
):
    blocks, lanes = codes_s.shape[::-1]
    width = chunk0_ref.shape[0]
    rows = 3 * width
    vocab = chunk0_ref.shape[1]
    half = vocab // 2
    me = me_ref[0]
    columns = columns_ref[...]

    chunks[0] = chunk0_ref[...]
    chunks[1] = chunk1_ref[...]
    chunks[2] = chunk2_ref[...]
    parts = [chunks[(me + g * blocks) % 3] for g in range(3)]
    folded = jnp.concatenate([x[:, :half] for x in parts] + [x[:, half:] for x in parts], axis=0)

    entry = (lax.broadcasted_iota(jnp.int32, (16, blocks), 0).astype(F32) + 1.0).astype(BF16)

    def look_up(positions):
        found = []
        hots = []
        for p in positions:
            code = codes_s[p : p + 1, :]
            found.append(code)
            size = jnp.broadcast_to(jnp.abs(code), (16, blocks)).astype(BF16)
            equal = [jnp.where(entry == size - BF16(r), BF16(1), BF16(0)).astype(BF16) for r in range(0, half, 16)]
            hots.append(jnp.concatenate(equal, axis=0))
        both = dot(folded, jnp.concatenate(hots, axis=1))
        for h, p in enumerate(positions):
            here = both[:, h * blocks : (h + 1) * blocks]
            mixed[(p + 8) * rows : (p + 9) * rows, :] = jnp.where(found[h] < 0.0, here[rows:], here[:rows])

    def short_filter(positions):
        for c in range(0, width, 8):
            taps = [
                [jnp.broadcast_to(columns[c : c + 8, 8 * g + i : 8 * g + i + 1], (8, blocks)) for i in range(tap_count)]
                for g in range(3)
            ]

            def at(p, g):
                begin = (p + 8) * rows + g * width + c
                return mixed[begin : begin + 8, :]

            window = [[at(positions[0] - i, g) for i in range(1, tap_count)] for g in range(3)]
            for p in positions:
                total = []
                for g in range(3):
                    here = at(p, g)
                    value = taps[g][0] * here
                    for i in range(1, tap_count):
                        value = value + taps[g][i] * window[g][i - 1]
                    total.append(value)
                    window[g] = [here] + window[g][:-1]
                gate[p * pitch + c : p * pitch + c + 8, :] = total[0]
                signal[p * pitch + c : p * pitch + c + 8, :] = total[1] * total[2]

    steps = [range(p, p + AT_ONCE) for p in range(0, lanes, AT_ONCE)]
    look_up(steps[-1])
    block = lax.broadcasted_iota(jnp.int32, (rows, blocks), 1)
    for i in range(1, tap_count):
        last = mixed[(lanes + 8 - i) * rows : (lanes + 9 - i) * rows, :]
        mixed[(8 - i) * rows : (9 - i) * rows, :] = jnp.where(block == 0, 0.0, pltpu.roll(last, 1, 1))
    for k, step in enumerate(steps):
        if k == 0:
            look_up(step)
        if k + 1 < len(steps) - 1:
            look_up(steps[k + 1])
        short_filter(step)

    cos, sin, first, second, second_back, first_back = matrices(constants_ref)

    for begin in range(0, width, TOGETHER):
        signals = [channel(signal, begin + h, pitch).T for h in range(TOGETHER)]
        z = forward(signals, cos, sin, first, second)
        products = []
        for h in range(TOGETHER):
            s = z[h * blocks : (h + 1) * blocks]
            f = spectrum_ref[(begin + h) * blocks : (begin + h + 1) * blocks, :].astype(F32)
            s_re, s_im, f_re, f_im = s[:, :lanes], s[:, lanes:], f[:, :lanes], f[:, lanes:]
            products.append(
                jnp.concatenate([f_re * s_re - f_im * s_im, f_re * s_im + f_im * s_re], axis=1).astype(BF16)
            )
        back = dot(jnp.concatenate(products, axis=0), second_back)
        unturned = []
        for h in range(TOGETHER):
            re = back[h * blocks : (h + 1) * blocks, :lanes]
            im = back[h * blocks : (h + 1) * blocks, lanes:]
            unturned.append(jnp.concatenate([re * cos - im * sin, im * cos + re * sin], axis=0).astype(BF16))
        for j in range(0, TOGETHER, 2):
            y = dot(first_back, jnp.concatenate(unturned[j : j + 2], axis=1))
            for h in range(2):
                c = begin + j + h
                inner = y[:, h * lanes : (h + 1) * lanes] + columns[c : c + 1, 24:25] * signals[j + h]
                long_s[pl.ds(c, blocks, stride=pitch), :] = channel(gate, c, pitch).T * inner

    def round_step(b, carry):
        out_ref[pl.ds(pl.multiple_of(b * width, width), width), :] = long_s[pl.ds(b * pitch, width), :].astype(BF16)
        return carry

    lax.fori_loop(0, blocks, round_step, 0, unroll=8)


def conv_call(me, arrived, chunk0, chunk1, chunk2, columns, constants, tap_count):
    blocks, rows_in, positions = arrived.shape
    width, vocab = chunk0.shape
    rows = 3 * width
    pitch = width + 1
    vmem = pl.BlockSpec(memory_space=pltpu.VMEM)
    spectrum, codes = pl.pallas_call(
        functools.partial(filter_kernel, pitch=pitch),
        in_specs=[vmem] * 2,
        out_specs=[vmem] * 2,
        out_shape=[
            jax.ShapeDtypeStruct((width * blocks, 2 * positions), BF16),
            jax.ShapeDtypeStruct((positions, blocks), F32),
        ],
        scratch_shapes=[pltpu.VMEM((blocks * pitch, positions), F32)],
        compiler_params=pltpu.CompilerParams(vmem_limit_bytes=16 * 1024 * 1024),
        name="filter_spectrum",
    )(arrived, constants)
    return pl.pallas_call(
        functools.partial(conv_kernel, tap_count=tap_count, pitch=pitch),
        in_specs=[pl.BlockSpec(memory_space=pltpu.SMEM)] + [vmem] * 7,
        out_specs=vmem,
        out_shape=jax.ShapeDtypeStruct((blocks * width, positions), BF16),
        scratch_shapes=[
            pltpu.VMEM((positions * pitch, blocks), F32),
            pltpu.VMEM((positions * pitch, blocks), F32),
            pltpu.VMEM(((positions + 8) * rows, blocks), F32),
            pltpu.VMEM((blocks * pitch, positions), F32),
            pltpu.VMEM((3, width, vocab), BF16),
        ],
        compiler_params=pltpu.CompilerParams(vmem_limit_bytes=32 * 1024 * 1024),
        name="convolution",
    )(me, spectrum, codes, chunk0, chunk1, chunk2, columns, constants)


def local(token_ids, embedding, norm_gain, w_in, short_taps, long_filter, skip_gain):
    devices = lax.axis_size(AXES)
    me = lax.axis_index(AXES)
    positions, channels = long_filter.shape
    width = channels // devices
    vocab = embedding.shape[0]
    half = vocab // 2
    blocks = devices
    rows = 3 * width
    constants = transform_tables(blocks, positions)

    vmem = pl.BlockSpec(memory_space=pltpu.VMEM)
    hbm = pl.BlockSpec(memory_space=pltpu.HBM)
    sent = pl.pallas_call(
        functools.partial(pack_kernel, half=half),
        in_specs=[hbm, hbm],
        out_specs=vmem,
        out_shape=jax.ShapeDtypeStruct((devices, width + 1, positions), BF16),
        scratch_shapes=[
            pltpu.VMEM((positions, channels), F32),
            pltpu.VMEM((1, positions), jnp.int32),
            pltpu.SemaphoreType.DMA((PIECES + 1,)),
        ],
        compiler_params=pltpu.CompilerParams(vmem_limit_bytes=PACK_VMEM * 1024 * 1024),
        name="pack",
    )(long_filter, token_ids[None])
    arrived = lax.all_to_all(sent, AXES, split_axis=0, concat_axis=0, tiled=True)

    block = ((3 * me + 1) % devices)[None].astype(jnp.int32)
    *own, columns = pl.pallas_call(
        table_kernel,
        in_specs=[pl.BlockSpec(memory_space=pltpu.SMEM), vmem, vmem, vmem, hbm, hbm],
        out_specs=[vmem] * 4,
        out_shape=[jax.ShapeDtypeStruct((width, vocab), BF16)] * 3 + [jax.ShapeDtypeStruct((width, LANES), F32)],
        scratch_shapes=[
            pltpu.VMEM((LANES, embedding.shape[1]), BF16),
            pltpu.VMEM((8, embedding.shape[1]), F32),
            pltpu.VMEM((LANES, LANES), F32),
            pltpu.SemaphoreType.DMA((4,)),
        ],
        compiler_params=pltpu.CompilerParams(vmem_limit_bytes=TABLE_VMEM * 1024 * 1024),
        name="table",
    )(block, embedding, norm_gain[None], w_in.T, short_taps, skip_gain.reshape(channels // LANES, LANES))
    inverse = pow(3, -1, devices)
    moved = [
        lax.ppermute(own[1 + j], AXES, [(d, (d + j * inverse) % devices) for d in range(devices)]) for j in (-1, 1)
    ]
    chunks = [moved[0], own[1], moved[1]]

    out = conv_call(block, arrived, *chunks, columns, constants, short_taps.shape[0])
    received = lax.all_to_all(
        out.reshape(devices, width, positions), AXES, split_axis=0, concat_axis=0, tiled=True
    )
    return pl.pallas_call(
        unpack_kernel,
        in_specs=[vmem],
        out_specs=hbm,
        out_shape=jax.ShapeDtypeStruct((positions, channels), BF16),
        scratch_shapes=[pltpu.VMEM((positions, channels), BF16), pltpu.SemaphoreType.DMA((4,))],
        compiler_params=pltpu.CompilerParams(vmem_limit_bytes=16 * 1024 * 1024),
        name="unpack",
    )(received)


def solution(mesh):
    in_specs = (
        P(AXES),
        P(),
        P(),
        P(None, AXES),
        P(),
        P(AXES, None),
        P(),
    )
    out_specs = P(AXES, None)
    return jax.shard_map(local, mesh=mesh, in_specs=in_specs, out_specs=out_specs, check_vma=False)
```
